256 devices in a mesh: ed: 64 (over y, z, core), tp: 4 (over x).
Axes of the slice: x: 4, y: 4, z: 8, core: 2. Of those that a mesh axis runs over, the one named last changes fastest.
Arguments:
- layer_activations_input: bfloat16 [8192, 3072], P('ed', 'tp'), may hold values from -6 to 6
- output_gradient: bfloat16 [8192, 3072], P('ed', 'tp'), may hold values from -2 to 2
- specialist_choices_matrix: int32 [8192, 2], P('ed'), may hold values from 0 to 7, all different within a row
- mixing_coefficients: float32 [8192, 2], P('ed'), may hold values from 0.1 to 1
- quota_table: int32 [64, 8], P('ed'), may hold values from 4 to 12, as said below
- gating_matrix: bfloat16 [3072, 131072], P(None, ('ed', 'tp')), may hold values from -0.109375 to 0.109375
- widening_matrix: bfloat16 [3072, 131072], P(None, ('ed', 'tp')), may hold values from -0.109375 to 0.109375
- contracting_matrix: bfloat16 [131072, 3072], P(('ed', 'tp')), may hold values from -0.046875 to 0.046875
Outputs:
- token_grads: bfloat16 [8192, 3072], P('ed', 'tp')
- gate_grads: float32 [8192, 2], P('ed')
The draws below stay inside these ranges and needn't reach their ends.
Inputs may be any that keep to these rules, and one draw needn't show every extreme that they name: quota_table[s, e] is a multiple of 4; in every source block one expert (a low capacity: most assignments are dropped, as if the layer saw many more tokens at capacity factor about 1) has capacity 12.
All inputs are finite; a program needn't handle non-finite values.
Results may differ from the reference program's by a relative error of at most 0.011.
Values may be sent and summed in bfloat16 or wider, within the bound.
No kernel may reach another device: no remote copies, remote signals or barrier semaphores. Data moves between devices by JAX's collectives and lax.ppermute only.
A program may use at most 128 MiB of HBM per device.

```python
import jax
import jax.numpy as jnp
from jax import lax

D = 3072
FFW = 16384
EXPERTS = 8
TOP = 2
TOK_DEV = 128
CAP = 12
TOKENS = 8192
N_ED = 64


def draw_quota_table(key, part):
    key = jax.random.fold_in(key, 11)
    base_key, row_key = jax.random.split(key)
    drawn = jax.random.randint(base_key, (N_ED, EXPERTS), 1, CAP // 4 + 1, dtype=jnp.int32) * 4
    full_column = jax.random.randint(row_key, (N_ED, 1), 0, EXPERTS, dtype=jnp.int32)
    is_full = full_column == jnp.arange(EXPERTS, dtype=jnp.int32)[None, :]
    return jnp.where(is_full, CAP, drawn).astype(jnp.int32)


def level_of(key, extent, pieces, least, high):
    loudness, own = 1.0, jax.random.fold_in(key, 6)
    for axis_at, shards_of in pieces:
        draws = jnp.exp(jax.random.uniform(jax.random.fold_in(own, axis_at), (shards_of,), jnp.float32, least / len(pieces), high / len(pieces)))
        loudness = loudness * jnp.repeat(draws, extent[axis_at] // shards_of).reshape([-1 if axis == axis_at else 1 for axis in range(len(extent))])
    return loudness


def choose_distinct(stream_key, rows, amount, top, lift):
    order = jax.random.permutation(jax.random.fold_in(stream_key, 1), amount)
    pull = order
    for power in range(3):
        pull = pull * pull // amount
    pull = pull * lift // amount
    tickets = jax.random.randint(jax.random.fold_in(stream_key, 2), (rows, amount), 0, 4096) + pull
    sure = jax.random.permutation(jax.random.fold_in(stream_key, 3), rows)[jnp.arange(amount) % rows]
    tickets = jnp.where(jnp.arange(rows)[:, None] == sure[None, :], 1 << 14, tickets)
    priority = tickets * amount + jnp.arange(amount)
    return lax.top_k(priority.astype(jnp.int32), top)[1].astype(jnp.int32)


def noise(stream_key, dims, width, most, cuts=(), held_as=jnp.bfloat16):
    values = width * jax.random.normal(stream_key, dims, jnp.float32)
    if cuts:
        values = values * level_of(stream_key, dims, cuts, -0.22, 0.18)
    return jnp.clip(values, -most, most).astype(held_as)


def setup_inputs(seed: int = 0) -> dict:
    key_list = jax.random.split(jax.random.key(seed), 9)
    return {
        "layer_activations_input": noise(key_list[0], (TOKENS, D), 1.0, 6.0, ((0, 64), (1, 4))),
        "output_gradient": noise(key_list[1], (TOKENS, D), 0.15, 2.0, ((0, 64), (1, 4))),
        "specialist_choices_matrix": choose_distinct(key_list[2], TOKENS, EXPERTS, TOP, 4096),
        "mixing_coefficients": jnp.clip(0.1 + 0.9 * jax.random.uniform(key_list[3], (TOKENS, TOP), jnp.float32) ** level_of(key_list[3], (TOKENS, TOP), ((0, 64),), -0.2, 0.2), 0.1, 1.0),
        "quota_table": draw_quota_table(jax.random.fold_in(key_list[8], 71), 0),
        "gating_matrix": noise(key_list[5], (D, EXPERTS * FFW), D ** -0.5, 0.109375, ((1, 256),)),
        "widening_matrix": noise(key_list[6], (D, EXPERTS * FFW), D ** -0.5, 0.109375, ((1, 256),)),
        "contracting_matrix": noise(key_list[7], (EXPERTS * FFW, D), FFW ** -0.5, 0.046875, ((0, 256),)),
    }


def seat_positions(specialist_choices_matrix, capacity_row):
    flat_ids = specialist_choices_matrix.reshape(-1)
    onehot = (flat_ids[:, None] == jnp.arange(EXPERTS, dtype=jnp.int32)[None, :]).astype(jnp.int32)
    before = jnp.sum((jnp.cumsum(onehot, axis=0) - onehot) * onehot, axis=1)
    allowed = jnp.sum(onehot * capacity_row[None, :], axis=1)
    number = jnp.where(before < allowed, flat_ids * CAP + before, -1)
    return number.reshape(specialist_choices_matrix.shape)


def reference(layer_activations_input, output_gradient, specialist_choices_matrix, mixing_coefficients, quota_table, gating_matrix, widening_matrix, contracting_matrix):
    tile_numbers = specialist_choices_matrix.reshape(N_ED, TOK_DEV, TOP)
    block_weights = mixing_coefficients.reshape(N_ED, TOK_DEV, TOP)
    rank_numbers = jax.vmap(seat_positions)(tile_numbers, quota_table)
    positions = jnp.arange(TOK_DEV, dtype=jnp.int32)
    choice_index = jnp.arange(TOP, dtype=jnp.int32)
    token_sums = jnp.zeros((TOKENS, D), jnp.float32)
    gate_grads = jnp.zeros((TOKENS, TOP), jnp.float32)
    for expert in range(EXPERTS):
        wanted = expert * CAP + jnp.arange(CAP, dtype=jnp.int32)
        matches = rank_numbers[:, None, :, :] == wanted[None, :, None, None]
        token_hit = jnp.any(matches, axis=3)
        occupied = jnp.any(token_hit, axis=2).reshape(-1)
        local_token = jnp.sum(jnp.where(token_hit, positions[None, None, :], 0), axis=2)
        pick_slot = jnp.sum(jnp.where(matches, choice_index, 0), axis=(2, 3)).reshape(-1)
        slot_weight = jnp.sum(jnp.where(matches, block_weights[:, None, :, :], 0.0), axis=(2, 3)).reshape(-1)
        source_rows = (jnp.arange(N_ED, dtype=jnp.int32)[:, None] * TOK_DEV + local_token).reshape(-1).astype(jnp.int32)
        live_rows = occupied[:, None]
        rows_x = jnp.where(live_rows, layer_activations_input[source_rows], 0)
        rows_d = jnp.where(live_rows, output_gradient[source_rows], 0)
        w_gate = gating_matrix[:, expert * FFW:(expert + 1) * FFW]
        w_up = widening_matrix[:, expert * FFW:(expert + 1) * FFW]
        w_down = contracting_matrix[expert * FFW:(expert + 1) * FFW, :]
        pre_gate = jnp.dot(rows_x, w_gate, preferred_element_type=jnp.float32)
        pre_up = jnp.dot(rows_x, w_up, preferred_element_type=jnp.float32)
        sigmoid_gate = jax.nn.sigmoid(pre_gate)
        swish = pre_gate * sigmoid_gate
        activation = (swish * pre_up).astype(jnp.bfloat16)
        back_act = lax.dot_general(rows_d, w_down, (((1,), (1,)), ((), ())), preferred_element_type=jnp.float32)
        partial_dot = jnp.sum(activation.astype(jnp.float32) * back_act, axis=1)
        grad_gate = (back_act * pre_up * sigmoid_gate * (1.0 + pre_gate * (1.0 - sigmoid_gate))).astype(jnp.bfloat16)
        grad_up = (back_act * swish).astype(jnp.bfloat16)
        back_rows = jnp.dot(grad_gate, w_gate.T, preferred_element_type=jnp.float32) + jnp.dot(grad_up, w_up.T, preferred_element_type=jnp.float32)
        token_sums = token_sums.at[source_rows].add(slot_weight[:, None] * back_rows)
        gate_grads = gate_grads.at[source_rows, pick_slot].add(jnp.where(occupied, partial_dot, 0.0))
    return token_sums.astype(jnp.bfloat16), gate_grads
```

```python
import functools

import jax
import jax.numpy as jnp
from jax import lax
from jax.experimental import pallas as pl
from jax.experimental.pallas import tpu as pltpu
from jax.sharding import PartitionSpec as P

EXPERTS = 8
CAP = 12
PAD = 16
SLOTS = EXPERTS * CAP
BLOCK = 768
GROUPS = ((0, 1, 2, 3),)
OFFSETS = (0, 3, 1, 2)
HIDDEN_STEP = 256


def seat_positions(specialist_choices_matrix, capacity_row):
    flat_ids = specialist_choices_matrix.reshape(-1)
    onehot = (flat_ids[:, None] == jnp.arange(EXPERTS, dtype=jnp.int32)[None, :]).astype(jnp.int32)
    before = jnp.sum((jnp.cumsum(onehot, axis=0) - onehot) * onehot, axis=1)
    allowed = jnp.sum(onehot * capacity_row[None, :], axis=1)
    number = jnp.where(before < allowed, flat_ids * PAD + before, -1)
    return number.reshape(specialist_choices_matrix.shape)


def along_x(value, step):
    return lax.ppermute(value, "tp", [(i, (i + step) % 4) for i in range(4)])


def along_z(value, flip):
    return lax.ppermute(value, "ed", [(i, i ^ (flip * 2)) for i in range(64)])


def across_cores(value):
    return lax.ppermute(value, "ed", [(i, i ^ 1) for i in range(64)])


def among_experts(value):
    groups = [[expert * 8 + place for expert in range(EXPERTS)] for place in range(8)]
    return lax.all_to_all(
        value, "ed", split_axis=0, concat_axis=0, tiled=True, axis_index_groups=groups
    )


def expert_body(pieces, place_ref, *refs):
    piece_refs = refs[: 5 * pieces]
    weights = (refs[5 * pieces : 5 * pieces + 3], refs[5 * pieces + 3 : 5 * pieces + 6])
    outs = refs[5 * pieces + 6 : 5 * pieces + 10]
    dot_ref = refs[5 * pieces + 10]
    xs, ys, acc = refs[5 * pieces + 11 :]
    step = pl.program_id(0)

    @pl.when(step == 0)
    def _():
        for piece in range(pieces):
            own, left, right, far_x, far_d = piece_refs[5 * piece : 5 * piece + 5]
            rows = pl.ds(piece * SLOTS, SLOTS)
            for k, block in enumerate((own, left, right)):
                xs[k, rows, :] = block[:SLOTS, :]
                ys[k, rows, :] = block[SLOTS:, :]
            xs[3, rows, :] = far_x[...]
            ys[3, rows, :] = far_d[...]
        dot_ref[...] = jnp.zeros_like(dot_ref)

    place = place_ref[0]
    starts = [pl.multiple_of(((place + off) % 4) * BLOCK, BLOCK) for off in OFFSETS]
    f32 = jnp.float32
    transposed = (((1,), (1,)), ((), ()))
    grads = []
    dots = dot_ref[...]
    for gate_ref, up_ref, down_ref in weights:
        pre_gate = sum(
            jnp.dot(xs[k], gate_ref[pl.ds(starts[k], BLOCK), :], preferred_element_type=f32)
            for k in range(4)
        )
        pre_up = sum(
            jnp.dot(xs[k], up_ref[pl.ds(starts[k], BLOCK), :], preferred_element_type=f32)
            for k in range(4)
        )
        back_act = sum(
            lax.dot_general(
                ys[k], down_ref[:, pl.ds(starts[k], BLOCK)], transposed, preferred_element_type=f32
            )
            for k in range(4)
        )
        sigmoid_gate = jax.nn.sigmoid(pre_gate)
        swish = pre_gate * sigmoid_gate
        activation = (swish * pre_up).astype(jnp.bfloat16)
        product = activation.astype(f32) * back_act
        for lane in range(HIDDEN_STEP // 128):
            dots = dots + product[:, lane * 128 : (lane + 1) * 128]
        grads.append(
            (
                (back_act * pre_up * sigmoid_gate * (1.0 + pre_gate * (1.0 - sigmoid_gate))).astype(
                    jnp.bfloat16
                ),
                (back_act * swish).astype(jnp.bfloat16),
            )
        )
    dot_ref[...] = dots
    last = pl.num_programs(0) - 1
    for k in (3, 1, 2, 0):
        total = None
        for (grad_gate, grad_up), (gate_ref, up_ref, _) in zip(grads, weights):
            term = lax.dot_general(
                grad_gate, gate_ref[pl.ds(starts[k], BLOCK), :], transposed, preferred_element_type=f32
            ) + lax.dot_general(
                grad_up, up_ref[pl.ds(starts[k], BLOCK), :], transposed, preferred_element_type=f32
            )
            total = term if total is None else total + term

        @pl.when(step == 0)
        def _():
            acc[k] = total

        @pl.when(step == last)
        def _():
            outs[k][...] = (acc[k] + total).astype(outs[k].dtype)


def expert(place, pieces, own_weights, other_weights):
    count = len(pieces)
    rows = count * SLOTS
    whole = lambda shape: pl.BlockSpec(shape, lambda j: (0, 0))
    hidden = own_weights[0].shape[1]
    features = own_weights[0].shape[0]
    weight_specs = [
        pl.BlockSpec((features, HIDDEN_STEP), lambda j: (0, j)),
        pl.BlockSpec((features, HIDDEN_STEP), lambda j: (0, j)),
        pl.BlockSpec((HIDDEN_STEP, features), lambda j: (j, 0)),
    ]
    flat = [block for piece in pieces for block in piece]
    out_shape = [
        jax.ShapeDtypeStruct((rows, BLOCK), jnp.float32 if k == 0 else jnp.bfloat16) for k in range(4)
    ] + [jax.ShapeDtypeStruct((rows, 128), jnp.float32)]
    flops = 5 * 2 * rows * features * hidden * 2
    return pl.pallas_call(
        functools.partial(expert_body, count),
        grid=(hidden // HIDDEN_STEP,),
        in_specs=[pl.BlockSpec(memory_space=pltpu.SMEM)]
        + [whole(block.shape) for block in flat]
        + weight_specs
        + weight_specs,
        out_specs=[whole(s.shape) for s in out_shape],
        out_shape=out_shape,
        scratch_shapes=[
            pltpu.VMEM((4, rows, BLOCK), jnp.bfloat16),
            pltpu.VMEM((4, rows, BLOCK), jnp.bfloat16),
            pltpu.VMEM((4, rows, BLOCK), jnp.float32),
        ],
        compiler_params=pltpu.CompilerParams(vmem_limit_bytes=58 * 1024 * 1024),
        cost_estimate=pl.CostEstimate(
            flops=flops, bytes_accessed=6 * features * hidden * 2, transcendentals=rows * hidden * 2
        ),
        name="expert",
    )(place, *flat, *own_weights, *other_weights)


def local(
    layer_activations_input,
    output_gradient,
    specialist_choices_matrix,
    mixing_coefficients,
    quota_table,
    gating_matrix,
    widening_matrix,
    contracting_matrix,
):
    f32, bf16 = jnp.float32, jnp.bfloat16
    place = lax.axis_index("tp").astype(jnp.int32).reshape(1)
    own_weights = (gating_matrix, widening_matrix, contracting_matrix)
    other_weights = tuple(across_cores(w) for w in own_weights)

    numbers = seat_positions(specialist_choices_matrix, quota_table[0])
    row = jnp.arange(EXPERTS * 2 * CAP, dtype=jnp.int32)
    kind = (row // CAP) % 2
    seat = (row // (2 * CAP)) * PAD + row % CAP
    hit = jnp.any(numbers[None, :, :] == seat[:, None, None], axis=2)
    picker = jnp.concatenate(
        [hit & (kind == 0)[:, None], hit & (kind == 1)[:, None]], axis=1
    ).astype(bf16)
    both = jnp.concatenate([layer_activations_input, output_gradient], axis=0)
    payload = jnp.dot(picker, both, preferred_element_type=f32).astype(bf16)
    arrived = among_experts(payload.reshape(EXPERTS, 2 * CAP, BLOCK)).reshape(-1, BLOCK)
    goal = kind * SLOTS + (row // (2 * CAP)) * CAP + row % CAP
    sorter = (jnp.arange(2 * SLOTS, dtype=jnp.int32)[:, None] == goal[None, :]).astype(bf16)
    mine = jnp.dot(sorter, arrived, preferred_element_type=f32).astype(bf16)

    pieces = []
    for flip in range(4):
        own = mine if flip == 0 else along_z(mine, flip)
        left = along_x(own, 1)
        right = along_x(own, -1)
        far_x = along_x(left[:SLOTS], 1)
        far_d = along_x(right[SLOTS:], -1)
        pieces.append((own, left, right, far_x, far_d))

    sums = [None] * 4
    dots = [None] * 4
    for group in GROUPS:
        kept, to_left, to_right, to_far, lanes = expert(
            place, [pieces[flip] for flip in group], own_weights, other_weights
        )
        product = jnp.sum(lanes, axis=1).reshape(len(group), SLOTS)
        product = product + along_x(product, 1) + along_x(product, -1) + along_x(product, 2)
        total = (
            kept
            + along_x(to_right, 1).astype(f32)
            + along_x(to_left, -1).astype(f32)
            + along_x(to_far, 2).astype(f32)
        )
        for at, flip in enumerate(group):
            sums[flip] = total[at * SLOTS : (at + 1) * SLOTS]
            dots[flip] = product[at : at + 1]
    rows = sums[0]
    product = dots[0]
    for flip in range(1, 4):
        rows = rows + along_z(sums[flip].astype(bf16), flip).astype(f32)
        product = product + along_z(dots[flip], flip)

    product = product.reshape(EXPERTS, 1, CAP)
    high = product.astype(bf16)
    low = (product - high.astype(f32)).astype(bf16)
    tail = jnp.concatenate([high, low, jnp.zeros((EXPERTS, PAD - CAP - 2, CAP), bf16)], axis=1)
    tail = jnp.pad(tail, ((0, 0), (0, 0), (0, BLOCK - CAP)))
    home = among_experts(
        jnp.concatenate([rows.astype(bf16).reshape(EXPERTS, CAP, BLOCK), tail], axis=1)
    )
    slot_dot = home[:, CAP, :PAD].astype(f32) + home[:, CAP + 1, :PAD].astype(f32)
    slot_dot = slot_dot.reshape(-1)
    matches = numbers[None, :, :] == jnp.arange(EXPERTS * PAD, dtype=jnp.int32)[:, None, None]
    slot_weight = jnp.sum(jnp.where(matches, mixing_coefficients[None, :, :], 0.0), axis=2)
    token_sums = lax.dot_general(
        slot_weight,
        home.reshape(EXPERTS * PAD, BLOCK).astype(f32),
        (((0,), (0,)), ((), ())),
        precision=lax.Precision.HIGHEST,
        preferred_element_type=f32,
    )
    gate_grads = jnp.sum(jnp.where(matches, slot_dot[:, None, None], 0.0), axis=0)
    return (token_sums.astype(bf16), gate_grads)


def solution(mesh):
    in_specs = (
        P("ed", "tp"),
        P("ed", "tp"),
        P("ed", None),
        P("ed", None),
        P("ed", None),
        P(None, ("ed", "tp")),
        P(None, ("ed", "tp")),
        P(("ed", "tp"), None),
    )
    out_specs = (P("ed", "tp"), P("ed", None))
    return jax.shard_map(local, mesh=mesh, in_specs=in_specs, out_specs=out_specs, check_vma=False)
```

```python
import functools

import jax
import jax.numpy as jnp
from jax import lax
from jax.experimental import pallas as pl
from jax.experimental.pallas import tpu as pltpu
from jax.sharding import PartitionSpec as P

EXPERTS = 8
CAP = 12
BLOCK = 768
HIDDEN = 512
CHUNK = 256
PIECE = 4 * CAP
TAIL = 16
OFFSETS = (0, 3, 1, 2)


def ranks(flat_ids, capacity_row):
    onehot = (flat_ids[:, None] == jnp.arange(EXPERTS, dtype=jnp.int32)[None, :]).astype(jnp.int32)
    before = jnp.sum((jnp.cumsum(onehot, axis=0) - onehot) * onehot, axis=1)
    allowed = jnp.sum(onehot * capacity_row[None, :], axis=1)
    return before, before < allowed


def along_x(value, step):
    return lax.ppermute(value, "tp", [(i, (i + step) % 4) for i in range(4)])


def along_y(value, step):
    return lax.ppermute(value, "ed", [(i, (i + 16 * step) % 64) for i in range(64)])


def along_z(value, flip):
    return lax.ppermute(value, "ed", [(i, i ^ (flip * 2)) for i in range(64)])


def across_cores(value):
    return lax.ppermute(value, "ed", [(i, i ^ 1) for i in range(64)])


def expert_body(counts, place_ref, *refs):
    groups = len(counts)
    group_refs = refs[: 5 * groups]
    refs = refs[5 * groups :]
    outs = refs[6:10]
    xs, ys, gates, ups = refs[10:]
    weights = (refs[:3], refs[3:6])
    f32, bf16 = jnp.float32, jnp.bfloat16
    total_rows = sum(counts) * PIECE
    place = place_ref[0]
    starts = [pl.multiple_of(((place + off) % 4) * BLOCK, BLOCK) for off in OFFSETS]
    base = 0
    for at, count in enumerate(counts):
        own, left, right, far_low, far_high = group_refs[5 * at : 5 * at + 5]
        for piece in range(count):
            for kind, goal in enumerate((xs, ys)):
                line = (2 * piece + kind) * PIECE
                rows = slice(base, base + PIECE)
                for k, block in enumerate((own, left, right)):
                    goal[rows, pl.ds(starts[k], BLOCK)] = block[line : line + PIECE, :]
                half = count * PIECE
                far = far_low if line < half else far_high
                goal[rows, pl.ds(starts[3], BLOCK)] = far[line % half : line % half + PIECE, :]
            base += PIECE
    transposed = (((1,), (1,)), ((), ()))
    dots = jnp.zeros((total_rows, 128), f32)
    for side, (gate_ref, up_ref, down_ref) in enumerate(weights):
        for chunk in range(HIDDEN // CHUNK):
            columns = slice(chunk * CHUNK, (chunk + 1) * CHUNK)
            pre_gate = jnp.dot(xs[...], gate_ref[:, columns], preferred_element_type=f32)
            pre_up = jnp.dot(xs[...], up_ref[:, columns], preferred_element_type=f32)
            back_act = lax.dot_general(
                ys[...], down_ref[columns, :], transposed, preferred_element_type=f32
            )
            sigmoid_gate = jax.nn.sigmoid(pre_gate)
            swish = pre_gate * sigmoid_gate
            activation = (swish * pre_up).astype(bf16)
            product = activation.astype(f32) * back_act
            for lane in range(CHUNK // 128):
                dots = dots + product[:, lane * 128 : (lane + 1) * 128]
            at = slice(side * HIDDEN + chunk * CHUNK, side * HIDDEN + (chunk + 1) * CHUNK)
            gates[:, at] = (
                back_act * pre_up * sigmoid_gate * (1.0 + pre_gate * (1.0 - sigmoid_gate))
            ).astype(bf16)
            ups[:, at] = (back_act * swish).astype(bf16)
    square = (total_rows, total_rows)
    diagonal = lax.broadcasted_iota(jnp.int32, square, 0) == lax.broadcasted_iota(jnp.int32, square, 1)
    column = jnp.sum(dots, axis=1, keepdims=True)
    line = jnp.sum(jnp.where(diagonal, column, 0.0), axis=0, keepdims=True)
    line = jnp.broadcast_to(line, (TAIL, total_rows))
    row = lax.broadcasted_iota(jnp.int32, line.shape, 0)
    high = line.astype(bf16).astype(f32)
    for k in (3, 1, 2, 0):
        total = None
        for side, (gate_ref, up_ref, _) in enumerate(weights):
            for matrix, grads in ((gate_ref, gates), (up_ref, ups)):
                term = lax.dot_general(
                    grads[:, side * HIDDEN : (side + 1) * HIDDEN],
                    matrix[pl.ds(starts[k], BLOCK), :],
                    transposed,
                    preferred_element_type=f32,
                )
                total = term if total is None else total + term
        out = outs[k]
        out[:total_rows, :] = total.astype(out.dtype)
        out[total_rows:, :] = jnp.zeros((TAIL, BLOCK), out.dtype)
        if k == 0:
            tail = jnp.where(row == 0, line, 0.0)
        else:
            tail = jnp.where(row == 0, high, jnp.where(row == 1, line - high, 0.0))
        out[total_rows:, :total_rows] = tail.astype(out.dtype)


def expert(place, groups, counts, own_weights, other_weights):
    rows = sum(counts) * PIECE
    flat = [block for group in groups for block in group]
    vmem = pl.BlockSpec(memory_space=pltpu.VMEM)
    out_shape = [
        jax.ShapeDtypeStruct((rows + TAIL, BLOCK), jnp.float32 if k == 0 else jnp.bfloat16)
        for k in range(4)
    ]
    features = 4 * BLOCK
    return pl.pallas_call(
        functools.partial(expert_body, counts),
        in_specs=[pl.BlockSpec(memory_space=pltpu.SMEM)] + [vmem] * (len(flat) + 6),
        out_specs=[vmem] * 4,
        out_shape=out_shape,
        scratch_shapes=[
            pltpu.VMEM((rows, features), jnp.bfloat16),
            pltpu.VMEM((rows, features), jnp.bfloat16),
            pltpu.VMEM((rows, 2 * HIDDEN), jnp.bfloat16),
            pltpu.VMEM((rows, 2 * HIDDEN), jnp.bfloat16),
        ],
        compiler_params=pltpu.CompilerParams(vmem_limit_bytes=12 * 1024 * 1024),
        cost_estimate=pl.CostEstimate(
            flops=20 * rows * features * HIDDEN,
            bytes_accessed=12 * features * HIDDEN,
            transcendentals=rows * HIDDEN * 2,
        ),
        name="expert",
    )(place, *flat, *own_weights, *other_weights)


def onehot_rows(goal, source, dtype=jnp.bfloat16):
    return (goal[:, None] == source[None, :]).astype(dtype)


def local(
    layer_activations_input,
    output_gradient,
    specialist_choices_matrix,
    mixing_coefficients,
    quota_table,
    gating_matrix,
    widening_matrix,
    contracting_matrix,
):
    f32, bf16, i32 = jnp.float32, jnp.bfloat16, jnp.int32
    barrier = lax.optimization_barrier
    place = lax.axis_index("tp").astype(i32).reshape(1)
    own = lax.axis_index("ed").astype(i32)
    own_y, own_half = own // 16, (own // 8) % 2
    own_weights = (gating_matrix, widening_matrix, contracting_matrix)
    gating, place, own_y, own_half = barrier((gating_matrix, place, own_y, own_half))
    other_gate = across_cores(gating)

    flat_ids = specialist_choices_matrix.reshape(-1)
    before, kept = ranks(flat_ids, quota_table[0])
    steps = (flat_ids // 2 - own_y) % 4
    half = (flat_ids % 2) ^ own_half

    number = jnp.where(kept, steps * 48 + half * 24 + before, -1).reshape(-1, 2)
    row = jnp.arange(4 * 48, dtype=i32)
    kind = (row // CAP) % 2
    seat = row - kind * CAP
    hit = jnp.any(number[None, :, :] == seat[:, None, None], axis=2)
    picker = jnp.concatenate([hit & (kind == 0)[:, None], hit & (kind == 1)[:, None]], axis=1)
    both = jnp.concatenate([layer_activations_input, output_gradient], axis=0)
    payload = jnp.dot(picker.astype(bf16), both, preferred_element_type=f32).astype(bf16)
    payload, other_gate, widening, contracting = barrier(
        (payload, other_gate, widening_matrix, contracting_matrix)
    )
    other_up = across_cores(widening)
    other_down = across_cores(contracting)
    arrived = [payload[:48]] + [
        along_y(payload[48 * step : 48 * step + 48], step) for step in (1, 2, 3)
    ]
    arrived = jnp.concatenate(arrived, axis=0)
    arrived, other_up, other_down = barrier((arrived, other_up, other_down))
    other_weights = (other_gate, other_up, other_down)
    goal = (row // 24) % 2 * 96 + kind * PIECE + row // 48 * CAP + row % CAP
    sorter = onehot_rows(jnp.arange(192, dtype=i32), goal)
    sorted_rows = jnp.dot(sorter, arrived, preferred_element_type=f32).astype(bf16)
    same, other = sorted_rows[:96], sorted_rows[96:]

    def halves(block, left, right):
        middle = block.shape[0] // 2
        return along_x(left[:middle], 1), along_x(right[middle:], -1)

    near = [same, along_z(same, 1), along_z(same, 2), along_z(other, 6)]
    distant = [along_z(same, 3), along_z(other, 4), along_z(other, 5), along_z(other, 7)]
    block1 = jnp.concatenate(near, axis=0)
    left1, right1 = along_x(block1, 1), along_x(block1, -1)
    block2 = jnp.concatenate(distant, axis=0)
    block2, left1, right1 = barrier((block2, left1, right1))
    left2, right2 = along_x(block2, 1), along_x(block2, -1)
    far1 = halves(block1, left1, right1)
    first = expert(place, [(block1, left1, right1, *far1)], (4,), own_weights, other_weights)
    left2, right2, *first = barrier((left2, right2, *first))
    far2 = halves(block2, left2, right2)
    second = expert(place, [(block2, left2, right2, *far2)], (4,), own_weights, other_weights)

    back = [None] * 8
    for flips, (mine, to_left, to_right, to_far) in (((0, 1, 2, 6), first), ((3, 4, 5, 7), second)):
        rows = len(flips) * PIECE
        total = (
            mine
            + along_x(to_far, 2).astype(f32)
            + along_x(to_left, -1).astype(f32)
            + along_x(to_right, 1).astype(f32)
        )
        product = (total[rows, :rows] + total[rows + 1, :rows]).reshape(-1, 1, PIECE)
        high = product.astype(bf16).astype(f32)
        tail = jnp.concatenate(
            [high, product - high, jnp.zeros((len(flips), 6, PIECE), f32)], axis=1
        )
        tail = jnp.pad(tail, ((0, 0), (0, 0), (0, BLOCK - PIECE)))
        full = jnp.concatenate([total[:rows].reshape(-1, PIECE, BLOCK), tail], axis=1)
        for at, flip in enumerate(flips):
            back[flip] = full[at] if flip == 0 else along_z(full[at].astype(bf16), flip).astype(f32)
    same_rows = back[0] + back[1] + back[2] + back[3]
    other_rows = back[4] + back[5] + back[6] + back[7]

    dots = jnp.stack([same_rows[PIECE] + same_rows[PIECE + 1], other_rows[PIECE] + other_rows[PIECE + 1]])
    dots = dots[:, :PIECE].reshape(2, 4, CAP).transpose(1, 0, 2).reshape(4, 1, 2 * CAP)
    high = dots.astype(bf16)
    tail = jnp.concatenate(
        [high, (dots - high.astype(f32)).astype(bf16), jnp.zeros((4, 6, 2 * CAP), bf16)], axis=1
    )
    tail = jnp.pad(tail, ((0, 0), (0, 0), (0, BLOCK - 2 * CAP)))
    held = jnp.concatenate([same_rows[:PIECE], other_rows[:PIECE]], axis=0).astype(bf16)
    out_row = jnp.arange(96, dtype=i32)
    origin = (out_row // CAP) % 2 * PIECE + out_row // 24 * CAP + out_row % CAP
    returned = jnp.dot(
        onehot_rows(origin, jnp.arange(96, dtype=i32)), held, preferred_element_type=f32
    ).astype(bf16)
    returned = jnp.concatenate([returned.reshape(4, 24, BLOCK), tail], axis=1)
    home = jnp.stack([returned[0]] + [along_y(returned[step], -step) for step in (1, 2, 3)])

    slot_dot = (home[:, 24, : 2 * CAP].astype(f32) + home[:, 25, : 2 * CAP].astype(f32))
    slot_dot = jnp.pad(slot_dot, ((0, 0), (0, 8))).reshape(-1)
    place_home = jnp.where(kept, steps * 32 + half * CAP + before, -1).reshape(-1, 2)
    matches = place_home[None, :, :] == jnp.arange(128, dtype=i32)[:, None, None]
    slot_weight = jnp.sum(jnp.where(matches, mixing_coefficients[None, :, :], 0.0), axis=2)
    token_sums = lax.dot_general(
        slot_weight,
        home.reshape(128, BLOCK).astype(f32),
        (((0,), (0,)), ((), ())),
        precision=lax.Precision.HIGHEST,
        preferred_element_type=f32,
    )
    gate_grads = jnp.sum(jnp.where(matches, slot_dot[:, None, None], 0.0), axis=0)
    return (token_sums.astype(bf16), gate_grads)


def solution(mesh):
    in_specs = (
        P("ed", "tp"),
        P("ed", "tp"),
        P("ed", None),
        P("ed", None),
        P("ed", None),
        P(None, ("ed", "tp")),
        P(None, ("ed", "tp")),
        P(("ed", "tp"), None),
    )
    out_specs = (P("ed", "tp"), P("ed", None))
    return jax.shard_map(local, mesh=mesh, in_specs=in_specs, out_specs=out_specs, check_vma=False)
```

```python
import functools

import jax
import jax.numpy as jnp
from jax import lax
from jax.experimental import pallas as pl
from jax.experimental.pallas import tpu as pltpu
from jax.sharding import PartitionSpec as P

EXPERTS = 8
CAP = 12
BLOCK = 768
HIDDEN = 512
CHUNK = 256
PIECE = 4 * CAP
TAIL = 16
OFFSETS = (0, 3, 1, 2)


def along_x(value, step):
    return lax.ppermute(value, "tp", [(i, (i + step) % 4) for i in range(4)])


def along_y(value, step):
    return lax.ppermute(value, "ed", [(i, (i + 16 * step) % 64) for i in range(64)])


def along_z(value, flip):
    return lax.ppermute(value, "ed", [(i, i ^ (flip * 2)) for i in range(64)])


def across_cores(value):
    return lax.ppermute(value, "ed", [(i, i ^ 1) for i in range(64)])


def expert_body(counts, place_ref, *refs):
    groups = len(counts)
    group_refs = refs[: 5 * groups]
    refs = refs[5 * groups :]
    outs = refs[6:10]
    xs, ys, gates, ups = refs[10:]
    weights = (refs[:3], refs[3:6])
    f32, bf16 = jnp.float32, jnp.bfloat16
    total_rows = sum(counts) * PIECE
    place = place_ref[0]
    starts = [pl.multiple_of(((place + off) % 4) * BLOCK, BLOCK) for off in OFFSETS]
    base = 0
    for at, count in enumerate(counts):
        own, left, right, far_low, far_high = group_refs[5 * at : 5 * at + 5]
        for piece in range(count):
            for kind, goal in enumerate((xs, ys)):
                line = (2 * piece + kind) * PIECE
                rows = slice(base, base + PIECE)
                for k, block in enumerate((own, left, right)):
                    goal[rows, pl.ds(starts[k], BLOCK)] = block[line : line + PIECE, :]
                half = count * PIECE
                far = far_low if line < half else far_high
                goal[rows, pl.ds(starts[3], BLOCK)] = far[line % half : line % half + PIECE, :]
            base += PIECE
    transposed = (((1,), (1,)), ((), ()))
    dots = jnp.zeros((total_rows, 128), f32)
    for side, (gate_ref, up_ref, down_ref) in enumerate(weights):
        for chunk in range(HIDDEN // CHUNK):
            columns = slice(chunk * CHUNK, (chunk + 1) * CHUNK)
            pre_gate = jnp.dot(xs[...], gate_ref[:, columns], preferred_element_type=f32)
            pre_up = jnp.dot(xs[...], up_ref[:, columns], preferred_element_type=f32)
            back_act = lax.dot_general(
                ys[...], down_ref[columns, :], transposed, preferred_element_type=f32
            )
            sigmoid_gate = jax.nn.sigmoid(pre_gate)
            swish = pre_gate * sigmoid_gate
            activation = (swish * pre_up).astype(bf16)
            product = activation.astype(f32) * back_act
            for lane in range(CHUNK // 128):
                dots = dots + product[:, lane * 128 : (lane + 1) * 128]
            at = slice(side * HIDDEN + chunk * CHUNK, side * HIDDEN + (chunk + 1) * CHUNK)
            gates[:, at] = (
                back_act * pre_up * sigmoid_gate * (1.0 + pre_gate * (1.0 - sigmoid_gate))
            ).astype(bf16)
            ups[:, at] = (back_act * swish).astype(bf16)
    square = (total_rows, total_rows)
    diagonal = lax.broadcasted_iota(jnp.int32, square, 0) == lax.broadcasted_iota(jnp.int32, square, 1)
    column = jnp.sum(dots, axis=1, keepdims=True)
    line = jnp.sum(jnp.where(diagonal, column, 0.0), axis=0, keepdims=True)
    line = jnp.broadcast_to(line, (TAIL, total_rows))
    row = lax.broadcasted_iota(jnp.int32, line.shape, 0)
    high = line.astype(bf16).astype(f32)
    for k in (3, 1, 2, 0):
        total = None
        for side, (gate_ref, up_ref, _) in enumerate(weights):
            for matrix, grads in ((gate_ref, gates), (up_ref, ups)):
                term = lax.dot_general(
                    grads[:, side * HIDDEN : (side + 1) * HIDDEN],
                    matrix[pl.ds(starts[k], BLOCK), :],
                    transposed,
                    preferred_element_type=f32,
                )
                total = term if total is None else total + term
        out = outs[k]
        out[:total_rows, :] = total.astype(out.dtype)
        out[total_rows:, :] = jnp.zeros((TAIL, BLOCK), out.dtype)
        if k == 0:
            tail = jnp.where(row == 0, line, 0.0)
        else:
            tail = jnp.where(row == 0, high, jnp.where(row == 1, line - high, 0.0))
        out[total_rows:, :total_rows] = tail.astype(out.dtype)


def expert(place, groups, counts, own_weights, other_weights):
    rows = sum(counts) * PIECE
    flat = [block for group in groups for block in group]
    vmem = pl.BlockSpec(memory_space=pltpu.VMEM)
    out_shape = [
        jax.ShapeDtypeStruct((rows + TAIL, BLOCK), jnp.float32 if k == 0 else jnp.bfloat16)
        for k in range(4)
    ]
    features = 4 * BLOCK
    return pl.pallas_call(
        functools.partial(expert_body, counts),
        in_specs=[pl.BlockSpec(memory_space=pltpu.SMEM)] + [vmem] * (len(flat) + 6),
        out_specs=[vmem] * 4,
        out_shape=out_shape,
        scratch_shapes=[
            pltpu.VMEM((rows, features), jnp.bfloat16),
            pltpu.VMEM((rows, features), jnp.bfloat16),
            pltpu.VMEM((rows, 2 * HIDDEN), jnp.bfloat16),
            pltpu.VMEM((rows, 2 * HIDDEN), jnp.bfloat16),
        ],
        compiler_params=pltpu.CompilerParams(vmem_limit_bytes=12 * 1024 * 1024),
        cost_estimate=pl.CostEstimate(
            flops=20 * rows * features * HIDDEN,
            bytes_accessed=12 * features * HIDDEN,
            transcendentals=rows * HIDDEN * 2,
        ),
        name="expert",
    )(place, *flat, *own_weights, *other_weights)


SMALL = pltpu.CompilerParams(vmem_limit_bytes=6 * 1024 * 1024)
WIDE = BLOCK + 128
VMEM = pl.BlockSpec(memory_space=pltpu.VMEM)
SMEM = pl.BlockSpec(memory_space=pltpu.SMEM)


def seats(spot_ref, quota_ref, choices, steps, half, slot):
    f32, bf16 = jnp.float32, jnp.bfloat16
    expert_of = ((spot_ref[1] + steps) & 3) * 2 + (half ^ spot_ref[2])
    quota = jnp.zeros_like(expert_of)
    for index in range(EXPERTS):
        quota = jnp.where(expert_of == index, quota_ref[0, index], quota)
    chosen = [choices[:, k : k + 1] == expert_of for k in range(2)]
    taken = jnp.where(chosen[0], 1.0, jnp.where(chosen[1], 1.0, 0.0)).astype(bf16)
    tokens = choices.shape[0]
    square = (tokens, tokens)
    earlier = lax.broadcasted_iota(jnp.int32, square, 1) < lax.broadcasted_iota(jnp.int32, square, 0)
    before = jnp.dot(jnp.where(earlier, 1.0, 0.0).astype(bf16), taken, preferred_element_type=f32)
    seated = jnp.where(slot < quota, slot, -1).astype(f32) == before
    return [jnp.where(pick, jnp.where(seated, 1.0, 0.0), 0.0) for pick in chosen]


def front_body(spot_ref, quota_ref, choices_ref, x_ref, d_ref, *outs):
    lane = lax.broadcasted_iota(jnp.int32, (1, 192), 1)
    inner = lane % 24
    first, second = seats(
        spot_ref, quota_ref, choices_ref[...], lane // 48, (lane // 24) & 1, lane % CAP
    )
    hit = first + second
    tokens = (((0,), (0,)), ((), ()))
    rows = lax.dot_general(
        jnp.where(inner < CAP, hit, 0.0).astype(jnp.bfloat16),
        x_ref[...],
        tokens,
        preferred_element_type=jnp.float32,
    ) + lax.dot_general(
        jnp.where(inner >= CAP, hit, 0.0).astype(jnp.bfloat16),
        d_ref[...],
        tokens,
        preferred_element_type=jnp.float32,
    )
    for step in range(4):
        outs[step][...] = rows[48 * step : 48 * step + 48].astype(jnp.bfloat16)


def front(spot, quota, choices, x, d):
    return pl.pallas_call(
        front_body,
        in_specs=[SMEM, SMEM, VMEM, VMEM, VMEM],
        out_specs=[VMEM] * 4,
        out_shape=[jax.ShapeDtypeStruct((48, BLOCK), jnp.bfloat16)] * 4,
        compiler_params=SMALL,
        name="front",
    )(spot, quota, choices, x, d)


def sort_body(*refs):
    source = lax.broadcasted_iota(jnp.int32, (96, 48), 1)
    target = lax.broadcasted_iota(jnp.int32, (96, 48), 0)
    kind, slot = (source // CAP) & 1, source % CAP
    for half in range(2):
        total = 0.0
        for step in range(4):
            goal = kind * PIECE + step * CAP + slot
            pick = jnp.where(source // 24 == half, goal, -1) == target
            total = total + jnp.dot(
                jnp.where(pick, 1.0, 0.0).astype(jnp.bfloat16),
                refs[step][...],
                preferred_element_type=jnp.float32,
            )
        refs[4 + half][...] = total.astype(jnp.bfloat16)


def sort_rows(parts):
    return pl.pallas_call(
        sort_body,
        in_specs=[VMEM] * 4,
        out_specs=[VMEM] * 2,
        out_shape=[jax.ShapeDtypeStruct((96, BLOCK), jnp.bfloat16)] * 2,
        compiler_params=SMALL,
        name="sort_rows",
    )(*parts)


def tail_columns(product, rows):
    lane = lax.broadcasted_iota(jnp.int32, (rows, 128), 1)
    high = product.astype(jnp.bfloat16).astype(jnp.float32)
    return jnp.where(lane == 0, high, jnp.where(lane == 1, product - high, 0.0))


def collect_body(mine, to_far, to_left, to_right, *outs):
    f32 = jnp.float32
    rows = mine.shape[0] - TAIL
    total = (
        mine[...] + to_far[...].astype(f32) + to_left[...].astype(f32) + to_right[...].astype(f32)
    )
    square = (rows, rows)
    diagonal = lax.broadcasted_iota(jnp.int32, square, 0) == lax.broadcasted_iota(jnp.int32, square, 1)
    line = total[rows : rows + 1, :rows] + total[rows + 1 : rows + 2, :rows]
    column = jnp.sum(jnp.where(diagonal, line, 0.0), axis=1, keepdims=True)
    tail = tail_columns(column, rows)
    for at, out in enumerate(outs):
        part = slice(at * PIECE, (at + 1) * PIECE)
        out[:, :BLOCK] = total[part].astype(out.dtype)
        out[:, BLOCK:] = tail[part].astype(out.dtype)


def collect(blocks, types):
    return pl.pallas_call(
        collect_body,
        in_specs=[VMEM] * 4,
        out_specs=[VMEM] * len(types),
        out_shape=[jax.ShapeDtypeStruct((PIECE, WIDE), t) for t in types],
        compiler_params=SMALL,
        name="collect",
    )(*blocks)


def homeward_body(*refs):
    f32, bf16 = jnp.float32, jnp.bfloat16
    rows = []
    for half in range(2):
        total = sum(refs[4 * half + at][...].astype(f32) for at in range(4))
        product = total[:, BLOCK : BLOCK + 1] + total[:, BLOCK + 1 : BLOCK + 2]
        rows.append((total[:, :BLOCK].astype(bf16), tail_columns(product, PIECE).astype(bf16)))
    source = lax.broadcasted_iota(jnp.int32, (32, PIECE), 1)
    target = lax.broadcasted_iota(jnp.int32, (32, PIECE), 0)
    for step in range(4):
        out = refs[8 + step]
        picks = [
            jnp.where(
                jnp.where(source // CAP == step, half * CAP + source % CAP, -1) == target, 1.0, 0.0
            ).astype(bf16)
            for half in range(2)
        ]
        for part, lanes in ((0, slice(0, BLOCK)), (1, slice(BLOCK, WIDE))):
            out[:, lanes] = sum(
                jnp.dot(picks[half], rows[half][part], preferred_element_type=f32) for half in range(2)
            ).astype(bf16)


def homeward(parts):
    return pl.pallas_call(
        homeward_body,
        in_specs=[VMEM] * 8,
        out_specs=[VMEM] * 4,
        out_shape=[jax.ShapeDtypeStruct((32, WIDE), jnp.bfloat16)] * 4,
        compiler_params=SMALL,
        name="homeward",
    )(*parts)


def finish_body(spot_ref, quota_ref, choices_ref, mixing_ref, *refs):
    f32, bf16 = jnp.float32, jnp.bfloat16
    parts, (token_ref, gate_ref) = refs[:4], refs[4:]
    lane = lax.broadcasted_iota(jnp.int32, (1, 128), 1)
    inner = lane & 31
    half = jnp.where(inner < CAP, 0, 1)
    slot = jnp.where(inner < 2 * CAP, inner - half * CAP, 1 << 20)
    picks = seats(spot_ref, quota_ref, choices_ref[...], lane >> 5, half, slot)
    weight = picks[0] * mixing_ref[:, 0:1] + picks[1] * mixing_ref[:, 1:2]
    total = 0.0
    tails = jnp.concatenate([part[:, BLOCK:] for part in parts], axis=0)
    rows = jnp.concatenate([part[:, :BLOCK] for part in parts], axis=0)
    for _ in range(3):
        piece = weight.astype(bf16)
        weight = weight - piece.astype(f32)
        total = total + jnp.dot(piece, rows, preferred_element_type=f32)
    token_ref[...] = total.astype(bf16)
    for k in range(2):
        found = jnp.dot(picks[k].astype(bf16), tails, preferred_element_type=f32)
        gate_ref[:, k : k + 1] = found[:, 0:1] + found[:, 1:2]


def finish(spot, quota, choices, mixing, parts):
    return pl.pallas_call(
        finish_body,
        in_specs=[SMEM, SMEM] + [VMEM] * 6,
        out_specs=[VMEM] * 2,
        out_shape=[
            jax.ShapeDtypeStruct((128, BLOCK), jnp.bfloat16),
            jax.ShapeDtypeStruct((128, 2), jnp.float32),
        ],
        compiler_params=SMALL,
        name="finish",
    )(spot, quota, choices, mixing, *parts)


def local(
    layer_activations_input,
    output_gradient,
    specialist_choices_matrix,
    mixing_coefficients,
    quota_table,
    gating_matrix,
    widening_matrix,
    contracting_matrix,
):
    f32, bf16 = jnp.float32, jnp.bfloat16
    barrier = lax.optimization_barrier
    own = lax.axis_index("ed").astype(jnp.int32)
    spot = jnp.stack([lax.axis_index("tp").astype(jnp.int32), own >> 4, (own >> 3) & 1])
    own_weights = (gating_matrix, widening_matrix, contracting_matrix)
    gating, spot = barrier((gating_matrix, spot))
    other_gate = across_cores(gating)

    payload = front(
        spot, quota_table, specialist_choices_matrix, layer_activations_input, output_gradient
    )
    *payload, other_gate, widening, contracting = barrier(
        (*payload, other_gate, widening_matrix, contracting_matrix)
    )
    other_up = across_cores(widening)
    other_down = across_cores(contracting)
    arrived = [payload[0]] + [along_y(payload[step], step) for step in (1, 2, 3)]
    *arrived, other_up, other_down = barrier((*arrived, other_up, other_down))
    other_weights = (other_gate, other_up, other_down)
    same, other = sort_rows(arrived)

    def halves(block, left, right):
        middle = block.shape[0] // 2
        return along_x(left[:middle], 1), along_x(right[middle:], -1)

    near = [same, along_z(same, 1), along_z(same, 2), along_z(other, 6)]
    distant = [along_z(same, 3), along_z(other, 4), along_z(other, 5), along_z(other, 7)]
    block1 = jnp.concatenate(near, axis=0)
    left1, right1 = along_x(block1, 1), along_x(block1, -1)
    block2 = jnp.concatenate(distant, axis=0)
    block2, left1, right1 = barrier((block2, left1, right1))
    left2, right2 = along_x(block2, 1), along_x(block2, -1)
    far1 = halves(block1, left1, right1)
    first = expert(spot, [(block1, left1, right1, *far1)], (4,), own_weights, other_weights)
    left2, right2, *first = barrier((left2, right2, *first))
    far2 = halves(block2, left2, right2)
    second = expert(spot, [(block2, left2, right2, *far2)], (4,), own_weights, other_weights)

    def sum_over_x(parts):
        mine, to_left, to_right, to_far = parts
        return mine, along_x(to_far, 2), along_x(to_left, -1), along_x(to_right, 1)

    back1 = collect(sum_over_x(first), (f32, bf16, bf16, bf16))
    back1 = [back1[0]] + [along_z(part, flip) for part, flip in zip(back1[1:], (1, 2, 6))]
    back2 = collect(sum_over_x(second), (bf16,) * 4)
    back2 = [along_z(part, flip) for part, flip in zip(back2, (3, 4, 5, 7))]
    same_rows = (back1[0], back1[1], back1[2], back2[0])
    other_rows = (back1[3], *back2[1:])
    returned = homeward((*same_rows, *other_rows))
    home = [returned[0]] + [along_y(returned[step], -step) for step in (1, 2, 3)]
    return tuple(finish(spot, quota_table, specialist_choices_matrix, mixing_coefficients, home))


def solution(mesh):
    in_specs = (
        P("ed", "tp"),
        P("ed", "tp"),
        P("ed", None),
        P("ed", None),
        P("ed", None),
        P(None, ("ed", "tp")),
        P(None, ("ed", "tp")),
        P(("ed", "tp"), None),
    )
    out_specs = (P("ed", "tp"), P("ed", None))
    return jax.shard_map(local, mesh=mesh, in_specs=in_specs, out_specs=out_specs, check_vma=False)
```

```python
import functools

import jax
import jax.numpy as jnp
from jax import lax
from jax.experimental import pallas as pl
from jax.experimental.pallas import tpu as pltpu
from jax.sharding import PartitionSpec as P

EXPERTS = 8
CAP = 12
BLOCK = 768
HIDDEN = 512
CHUNK = 256
PIECE = 4 * CAP
TAIL = 16
OFFSETS = (0, 3, 1, 2)


def along_x(value, step):
    return lax.ppermute(value, "tp", [(i, (i + step) % 4) for i in range(4)])


def along_y(value, step):
    return lax.ppermute(value, "ed", [(i, (i + 16 * step) % 64) for i in range(64)])


def along_z(value, flip):
    return lax.ppermute(value, "ed", [(i, i ^ (flip * 2)) for i in range(64)])


def across_cores(value):
    return lax.ppermute(value, "ed", [(i, i ^ 1) for i in range(64)])


def expert_body(counts, place_ref, *refs):
    groups = len(counts)
    group_refs = refs[: 3 * groups]
    far_low, far_high = refs[3 * groups : 3 * groups + 2]
    refs = refs[3 * groups + 2 :]
    outs = refs[6:10]
    xs, ys, gates, ups = refs[10:]
    weights = (refs[:3], refs[3:6])
    f32, bf16 = jnp.float32, jnp.bfloat16
    total_rows = sum(counts) * PIECE
    place = place_ref[0]
    starts = [pl.multiple_of(((place + off) % 4) * BLOCK, BLOCK) for off in OFFSETS]
    base = 0
    for at, count in enumerate(counts):
        own, left, right = group_refs[3 * at : 3 * at + 3]
        half = count * PIECE
        origin = base
        for piece in range(count):
            for kind, goal in enumerate((xs, ys)):
                line = (2 * piece + kind) * PIECE
                rows = slice(base, base + PIECE)
                for k, block in enumerate((own, left, right)):
                    goal[rows, pl.ds(starts[k], BLOCK)] = block[line : line + PIECE, :]
                far = far_low if line < half else far_high
                from_row = origin + line % half
                goal[rows, pl.ds(starts[3], BLOCK)] = far[from_row : from_row + PIECE, :]
            base += PIECE
    transposed = (((1,), (1,)), ((), ()))
    dots = jnp.zeros((total_rows, 128), f32)
    for side, (gate_ref, up_ref, down_ref) in enumerate(weights):
        for chunk in range(HIDDEN // CHUNK):
            columns = slice(chunk * CHUNK, (chunk + 1) * CHUNK)
            pre_gate = jnp.dot(xs[...], gate_ref[:, columns], preferred_element_type=f32)
            pre_up = jnp.dot(xs[...], up_ref[:, columns], preferred_element_type=f32)
            back_act = lax.dot_general(
                ys[...], down_ref[columns, :], transposed, preferred_element_type=f32
            )
            sigmoid_gate = jax.nn.sigmoid(pre_gate)
            swish = pre_gate * sigmoid_gate
            activation = (swish * pre_up).astype(bf16)
            product = activation.astype(f32) * back_act
            for lane in range(CHUNK // 128):
                dots = dots + product[:, lane * 128 : (lane + 1) * 128]
            at = slice(side * HIDDEN + chunk * CHUNK, side * HIDDEN + (chunk + 1) * CHUNK)
            gates[:, at] = (
                back_act * pre_up * sigmoid_gate * (1.0 + pre_gate * (1.0 - sigmoid_gate))
            ).astype(bf16)
            ups[:, at] = (back_act * swish).astype(bf16)
    square = (total_rows, total_rows)
    diagonal = lax.broadcasted_iota(jnp.int32, square, 0) == lax.broadcasted_iota(jnp.int32, square, 1)
    column = jnp.sum(dots, axis=1, keepdims=True)
    line = jnp.sum(jnp.where(diagonal, column, 0.0), axis=0, keepdims=True)
    line = jnp.broadcast_to(line, (TAIL, total_rows))
    row = lax.broadcasted_iota(jnp.int32, line.shape, 0)
    high = line.astype(bf16).astype(f32)
    for k in (3, 1, 2, 0):
        total = None
        for side, (gate_ref, up_ref, _) in enumerate(weights):
            for matrix, grads in ((gate_ref, gates), (up_ref, ups)):
                term = lax.dot_general(
                    grads[:, side * HIDDEN : (side + 1) * HIDDEN],
                    matrix[pl.ds(starts[k], BLOCK), :],
                    transposed,
                    preferred_element_type=f32,
                )
                total = term if total is None else total + term
        out = outs[k]
        out[:total_rows, :] = total.astype(out.dtype)
        out[total_rows:, :] = jnp.zeros((TAIL, BLOCK), out.dtype)
        if k == 0:
            tail = jnp.where(row == 0, line, 0.0)
        else:
            tail = jnp.where(row == 0, high, jnp.where(row == 1, line - high, 0.0))
        out[total_rows:, :total_rows] = tail.astype(out.dtype)


def expert(place, groups, far, own_weights, other_weights):
    counts = tuple(group[0].shape[0] // (2 * PIECE) for group in groups)
    rows = sum(counts) * PIECE
    flat = [block for group in groups for block in group] + list(far)
    vmem = pl.BlockSpec(memory_space=pltpu.VMEM)
    out_shape = [
        jax.ShapeDtypeStruct((rows + TAIL, BLOCK), jnp.float32 if k == 0 else jnp.bfloat16)
        for k in range(4)
    ]
    features = 4 * BLOCK
    return pl.pallas_call(
        functools.partial(expert_body, counts),
        in_specs=[pl.BlockSpec(memory_space=pltpu.SMEM)] + [vmem] * (len(flat) + 6),
        out_specs=[vmem] * 4,
        out_shape=out_shape,
        scratch_shapes=[
            pltpu.VMEM((rows, features), jnp.bfloat16),
            pltpu.VMEM((rows, features), jnp.bfloat16),
            pltpu.VMEM((rows, 2 * HIDDEN), jnp.bfloat16),
            pltpu.VMEM((rows, 2 * HIDDEN), jnp.bfloat16),
        ],
        compiler_params=pltpu.CompilerParams(vmem_limit_bytes=8 * 1024 * 1024),
        cost_estimate=pl.CostEstimate(
            flops=20 * rows * features * HIDDEN,
            bytes_accessed=12 * features * HIDDEN,
            transcendentals=rows * HIDDEN * 2,
        ),
        name="expert",
    )(place, *flat, *own_weights, *other_weights)


SMALL = pltpu.CompilerParams(vmem_limit_bytes=4 * 1024 * 1024)
WIDE = BLOCK + 128
VMEM = pl.BlockSpec(memory_space=pltpu.VMEM)
SMEM = pl.BlockSpec(memory_space=pltpu.SMEM)


def as_column(line):
    square = (line.shape[1], line.shape[1])
    diagonal = lax.broadcasted_iota(jnp.int32, square, 0) == lax.broadcasted_iota(jnp.int32, square, 1)
    return jnp.sum(jnp.where(diagonal, line, jnp.zeros_like(line)), axis=1, keepdims=True)


def seats(spot_ref, quota_ref, choices, steps, half, slot):
    f32, bf16 = jnp.float32, jnp.bfloat16
    expert_of = ((spot_ref[1] + steps) & 3) * 2 + (half ^ spot_ref[2])
    quota = jnp.zeros_like(expert_of)
    for index in range(EXPERTS):
        quota = jnp.where(expert_of == index, quota_ref[0, index], quota)
    chosen = [as_column(choices[k : k + 1, :]) == expert_of for k in range(2)]
    taken = jnp.where(chosen[0], 1.0, jnp.where(chosen[1], 1.0, 0.0)).astype(bf16)
    tokens = choices.shape[1]
    square = (tokens, tokens)
    earlier = lax.broadcasted_iota(jnp.int32, square, 1) < lax.broadcasted_iota(jnp.int32, square, 0)
    before = jnp.dot(jnp.where(earlier, 1.0, 0.0).astype(bf16), taken, preferred_element_type=f32)
    seated = jnp.where(slot < quota, slot, -1).astype(f32) == before
    return [jnp.where(pick, jnp.where(seated, 1.0, 0.0), 0.0) for pick in chosen]


def front_body(spot_ref, quota_ref, choices_ref, x_hbm, d_hbm, *refs):
    outs, (x_ref, d_ref, arrivals) = refs[:4], refs[4:]
    copies = [
        pltpu.make_async_copy(x_hbm, x_ref, arrivals.at[0]),
        pltpu.make_async_copy(d_hbm, d_ref, arrivals.at[1]),
    ]
    for copy in copies:
        copy.start()
    lane = lax.broadcasted_iota(jnp.int32, (1, 192), 1)
    inner = lane % 24
    first, second = seats(
        spot_ref, quota_ref, choices_ref[...], lane // 48, (lane // 24) & 1, lane % CAP
    )
    hit = first + second
    tokens = (((0,), (0,)), ((), ()))
    for copy in copies:
        copy.wait()
    rows = lax.dot_general(
        jnp.where(inner < CAP, hit, 0.0).astype(jnp.bfloat16),
        x_ref[...],
        tokens,
        preferred_element_type=jnp.float32,
    ) + lax.dot_general(
        jnp.where(inner >= CAP, hit, 0.0).astype(jnp.bfloat16),
        d_ref[...],
        tokens,
        preferred_element_type=jnp.float32,
    )
    for step in range(4):
        outs[step][...] = rows[48 * step : 48 * step + 48].astype(jnp.bfloat16)


def front(spot, quota, choices, x, d):
    return pl.pallas_call(
        front_body,
        in_specs=[SMEM, SMEM, VMEM] + [pl.BlockSpec(memory_space=pltpu.HBM)] * 2,
        out_specs=[VMEM] * 4,
        out_shape=[jax.ShapeDtypeStruct((48, BLOCK), jnp.bfloat16)] * 4,
        scratch_shapes=[
            pltpu.VMEM(x.shape, x.dtype),
            pltpu.VMEM(d.shape, d.dtype),
            pltpu.SemaphoreType.DMA((2,)),
        ],
        compiler_params=SMALL,
        name="front",
    )(spot, quota, choices, x, d)


def hold_body(*refs):
    count = len(refs) // 2
    copies = [
        pltpu.make_async_copy(refs[at], refs[count + at], refs[-1].at[at]) for at in range(count)
    ]
    for copy in copies:
        copy.start()
    for copy in copies:
        copy.wait()


def hold(weights):
    return pl.pallas_call(
        hold_body,
        in_specs=[pl.BlockSpec(memory_space=pl.ANY)] * len(weights),
        out_specs=[VMEM] * len(weights),
        out_shape=[jax.ShapeDtypeStruct(w.shape, w.dtype) for w in weights],
        scratch_shapes=[pltpu.SemaphoreType.DMA((len(weights),))],
        compiler_params=SMALL,
        name="hold",
    )(*weights)


def sort_body(*refs):
    source = lax.broadcasted_iota(jnp.int32, (96, 48), 1)
    target = lax.broadcasted_iota(jnp.int32, (96, 48), 0)
    kind, slot = (source // CAP) & 1, source % CAP
    for half in range(2):
        total = 0.0
        for step in range(4):
            goal = kind * PIECE + step * CAP + slot
            pick = jnp.where(source // 24 == half, goal, -1) == target
            total = total + jnp.dot(
                jnp.where(pick, 1.0, 0.0).astype(jnp.bfloat16),
                refs[step][...],
                preferred_element_type=jnp.float32,
            )
        refs[4 + half][...] = total.astype(jnp.bfloat16)


def sort_rows(parts):
    return pl.pallas_call(
        sort_body,
        in_specs=[VMEM] * 4,
        out_specs=[VMEM] * 2,
        out_shape=[jax.ShapeDtypeStruct((96, BLOCK), jnp.bfloat16)] * 2,
        compiler_params=SMALL,
        name="sort_rows",
    )(*parts)


def tail_columns(product, rows):
    lane = lax.broadcasted_iota(jnp.int32, (rows, 128), 1)
    high = product.astype(jnp.bfloat16).astype(jnp.float32)
    return jnp.where(lane == 0, high, jnp.where(lane == 1, product - high, 0.0))


def collect_body(mine, to_far, to_left, to_right, *outs):
    f32 = jnp.float32
    rows = mine.shape[0] - TAIL
    total = (
        mine[...] + to_far[...].astype(f32) + to_left[...].astype(f32) + to_right[...].astype(f32)
    )
    square = (rows, rows)
    diagonal = lax.broadcasted_iota(jnp.int32, square, 0) == lax.broadcasted_iota(jnp.int32, square, 1)
    line = total[rows : rows + 1, :rows] + total[rows + 1 : rows + 2, :rows]
    column = jnp.sum(jnp.where(diagonal, line, 0.0), axis=1, keepdims=True)
    tail = tail_columns(column, rows)
    for at, out in enumerate(outs):
        part = slice(at * PIECE, (at + 1) * PIECE)
        out[:, :BLOCK] = total[part].astype(out.dtype)
        out[:, BLOCK:] = tail[part].astype(out.dtype)


def collect(blocks, types):
    return pl.pallas_call(
        collect_body,
        in_specs=[VMEM] * 4,
        out_specs=[VMEM] * len(types),
        out_shape=[jax.ShapeDtypeStruct((PIECE, WIDE), t) for t in types],
        compiler_params=SMALL,
        name="collect",
    )(*blocks)


def homeward_body(*refs):
    f32, bf16 = jnp.float32, jnp.bfloat16
    rows = []
    for half in range(2):
        total = sum(refs[4 * half + at][...].astype(f32) for at in range(4))
        product = total[:, BLOCK : BLOCK + 1] + total[:, BLOCK + 1 : BLOCK + 2]
        rows.append((total[:, :BLOCK].astype(bf16), tail_columns(product, PIECE).astype(bf16)))
    source = lax.broadcasted_iota(jnp.int32, (32, PIECE), 1)
    target = lax.broadcasted_iota(jnp.int32, (32, PIECE), 0)
    for step in range(4):
        out = refs[8 + step]
        picks = [
            jnp.where(
                jnp.where(source // CAP == step, half * CAP + source % CAP, -1) == target, 1.0, 0.0
            ).astype(bf16)
            for half in range(2)
        ]
        for part, lanes in ((0, slice(0, BLOCK)), (1, slice(BLOCK, WIDE))):
            out[:, lanes] = sum(
                jnp.dot(picks[half], rows[half][part], preferred_element_type=f32) for half in range(2)
            ).astype(bf16)


def homeward(parts):
    return pl.pallas_call(
        homeward_body,
        in_specs=[VMEM] * 8,
        out_specs=[VMEM] * 4,
        out_shape=[jax.ShapeDtypeStruct((32, WIDE), jnp.bfloat16)] * 4,
        compiler_params=SMALL,
        name="homeward",
    )(*parts)


def finish_body(spot_ref, quota_ref, choices_ref, mixing_ref, *refs):
    f32, bf16 = jnp.float32, jnp.bfloat16
    parts, (token_ref, gate_ref) = refs[:4], refs[4:]
    lane = lax.broadcasted_iota(jnp.int32, (1, 128), 1)
    inner = lane & 31
    half = jnp.where(inner < CAP, 0, 1)
    slot = jnp.where(inner < 2 * CAP, inner - half * CAP, 1 << 20)
    picks = seats(spot_ref, quota_ref, choices_ref[...], lane >> 5, half, slot)
    weight = sum(picks[k] * as_column(mixing_ref[k : k + 1, :]) for k in range(2))
    total = 0.0
    tails = jnp.concatenate([part[:, BLOCK:] for part in parts], axis=0)
    rows = jnp.concatenate([part[:, :BLOCK] for part in parts], axis=0)
    for _ in range(3):
        piece = weight.astype(bf16)
        weight = weight - piece.astype(f32)
        total = total + jnp.dot(piece, rows, preferred_element_type=f32)
    token_ref[...] = total.astype(bf16)
    for k in range(2):
        found = lax.dot_general(
            tails, picks[k].astype(bf16), (((0,), (1,)), ((), ())), preferred_element_type=f32
        )
        gate_ref[k : k + 1, :] = found[0:1, :] + found[1:2, :]


def finish(spot, quota, choices, mixing, parts):
    return pl.pallas_call(
        finish_body,
        in_specs=[SMEM, SMEM] + [VMEM] * 6,
        out_specs=[VMEM] * 2,
        out_shape=[
            jax.ShapeDtypeStruct((128, BLOCK), jnp.bfloat16),
            jax.ShapeDtypeStruct((2, 128), jnp.float32),
        ],
        compiler_params=SMALL,
        name="finish",
    )(spot, quota, choices, mixing, *parts)


def local(
    layer_activations_input,
    output_gradient,
    specialist_choices_matrix,
    mixing_coefficients,
    quota_table,
    gating_matrix,
    widening_matrix,
    contracting_matrix,
):
    f32, bf16 = jnp.float32, jnp.bfloat16
    barrier = lax.optimization_barrier
    own = lax.axis_index("ed").astype(jnp.int32)
    spot = jnp.stack([lax.axis_index("tp").astype(jnp.int32), own >> 4, (own >> 3) & 1])
    own_weights = (gating_matrix, widening_matrix, contracting_matrix)
    gating, spot = barrier((gating_matrix, spot))
    other_gate = across_cores(gating)

    choices = specialist_choices_matrix.T
    payload = front(spot, quota_table, choices, layer_activations_input, output_gradient)
    *payload, other_gate, widening, contracting = barrier(
        (*payload, other_gate, widening_matrix, contracting_matrix)
    )
    other_up = across_cores(widening)
    other_down = across_cores(contracting)
    arrived = [payload[0]] + [along_y(payload[step], step) for step in (1, 2, 3)]
    *arrived, other_up = barrier((*arrived, other_up))
    same, other = sort_rows(arrived)

    def opposite(left, right):
        middle = left.shape[0] // 2
        return along_x(left[:middle], 1), along_x(right[middle:], -1)

    near = [same, along_z(same, 1), along_z(other, 4), along_z(other, 5)]
    distant = [along_z(same, 2), along_z(same, 3), along_z(other, 6), along_z(other, 7)]
    block1 = jnp.concatenate(near, axis=0)
    block1, other_down, *held = barrier((block1, other_down, *hold(own_weights[1:])))
    own_weights = (gating_matrix, *held)
    left1, right1 = along_x(block1, 1), along_x(block1, -1)
    block2 = jnp.concatenate(distant, axis=0)
    block2, left1, right1 = barrier((block2, left1, right1))
    left2, right2 = along_x(block2, 1), along_x(block2, -1)
    groups1, far1 = [(block1, left1, right1)], opposite(left1, right1)
    other_weights = (other_gate, other_up, other_down)
    first = expert(spot, groups1, far1, own_weights, other_weights)
    left2, right2, *first = barrier((left2, right2, *first))
    groups2 = [(block2, left2, right2)]
    second = expert(spot, groups2, opposite(left2, right2), own_weights, other_weights)

    def sum_over_x(parts):
        mine, to_left, to_right, to_far = parts
        return mine, along_x(to_far, 2), along_x(to_left, -1), along_x(to_right, 1)

    back1 = collect(sum_over_x(first), (f32, bf16, bf16, bf16))
    back1 = [back1[0]] + [along_z(part, flip) for part, flip in zip(back1[1:], (1, 4, 5))]
    back2 = collect(sum_over_x(second), (bf16,) * 4)
    back2 = [along_z(part, flip) for part, flip in zip(back2, (2, 3, 6, 7))]
    same_rows = (back1[0], back1[1], back2[0], back2[1])
    other_rows = (back1[2], back1[3], back2[2], back2[3])
    returned = homeward((*same_rows, *other_rows))
    home = [returned[0]] + [along_y(returned[step], -step) for step in (1, 2, 3)]
    token_grads, gate_grads = finish(spot, quota_table, choices, mixing_coefficients.T, home)
    return token_grads, gate_grads.T


def solution(mesh):
    in_specs = (
        P("ed", "tp"),
        P("ed", "tp"),
        P("ed", None),
        P("ed", None),
        P("ed", None),
        P(None, ("ed", "tp")),
        P(None, ("ed", "tp")),
        P(("ed", "tp"), None),
    )
    out_specs = (P("ed", "tp"), P("ed", None))
    return jax.shard_map(local, mesh=mesh, in_specs=in_specs, out_specs=out_specs, check_vma=False)
```

```python
import functools

import jax
import jax.numpy as jnp
from jax import lax
from jax.experimental import pallas as pl
from jax.experimental.pallas import tpu as pltpu
from jax.sharding import PartitionSpec as P

EXPERTS = 8
CAP = 12
BLOCK = 768
HIDDEN = 512
CHUNK = 256
PIECE = 4 * CAP
TAIL = 16
OFFSETS = (0, 3, 1, 2)


def along_x(value, step):
    return lax.ppermute(value, "tp", [(i, (i + step) % 4) for i in range(4)])


def along_y(value, step):
    return lax.ppermute(value, "ed", [(i, (i + 16 * step) % 64) for i in range(64)])


def along_z(value, flip):
    return lax.ppermute(value, "ed", [(i, i ^ (flip * 2)) for i in range(64)])


def across_cores(value):
    return lax.ppermute(value, "ed", [(i, i ^ 1) for i in range(64)])


def expert_body(counts, place_ref, *refs):
    groups = len(counts)
    group_refs = refs[: 3 * groups]
    far_low, far_high = refs[3 * groups : 3 * groups + 2]
    refs = refs[3 * groups + 2 :]
    outs = refs[6:10]
    xs, ys, gates, ups = refs[10:]
    weights = (refs[:3], refs[3:6])
    f32, bf16 = jnp.float32, jnp.bfloat16
    total_rows = sum(counts) * PIECE
    place = place_ref[0]
    starts = [pl.multiple_of(((place + off) % 4) * BLOCK, BLOCK) for off in OFFSETS]
    base = 0
    for at, count in enumerate(counts):
        own, left, right = group_refs[3 * at : 3 * at + 3]
        half = count * PIECE
        origin = base
        for piece in range(count):
            for kind, goal in enumerate((xs, ys)):
                line = (2 * piece + kind) * PIECE
                rows = slice(base, base + PIECE)
                for k, block in enumerate((own, left, right)):
                    goal[rows, pl.ds(starts[k], BLOCK)] = block[line : line + PIECE, :]
                far = far_low if line < half else far_high
                from_row = origin + line % half
                goal[rows, pl.ds(starts[3], BLOCK)] = far[from_row : from_row + PIECE, :]
            base += PIECE
    transposed = (((1,), (1,)), ((), ()))
    dots = jnp.zeros((total_rows, 128), f32)
    for side, (gate_ref, up_ref, down_ref) in enumerate(weights):
        for chunk in range(HIDDEN // CHUNK):
            columns = slice(chunk * CHUNK, (chunk + 1) * CHUNK)
            pre_gate = jnp.dot(xs[...], gate_ref[:, columns], preferred_element_type=f32)
            pre_up = jnp.dot(xs[...], up_ref[:, columns], preferred_element_type=f32)
            back_act = lax.dot_general(
                ys[...], down_ref[columns, :], transposed, preferred_element_type=f32
            )
            sigmoid_gate = jax.nn.sigmoid(pre_gate)
            swish = pre_gate * sigmoid_gate
            activation = (swish * pre_up).astype(bf16)
            product = activation.astype(f32) * back_act
            for lane in range(CHUNK // 128):
                dots = dots + product[:, lane * 128 : (lane + 1) * 128]
            at = slice(side * HIDDEN + chunk * CHUNK, side * HIDDEN + (chunk + 1) * CHUNK)
            gates[:, at] = (
                back_act * pre_up * sigmoid_gate * (1.0 + pre_gate * (1.0 - sigmoid_gate))
            ).astype(bf16)
            ups[:, at] = (back_act * swish).astype(bf16)
    square = (total_rows, total_rows)
    diagonal = lax.broadcasted_iota(jnp.int32, square, 0) == lax.broadcasted_iota(jnp.int32, square, 1)
    column = jnp.sum(dots, axis=1, keepdims=True)
    line = jnp.sum(jnp.where(diagonal, column, 0.0), axis=0, keepdims=True)
    line = jnp.broadcast_to(line, (TAIL, total_rows))
    row = lax.broadcasted_iota(jnp.int32, line.shape, 0)
    high = line.astype(bf16).astype(f32)
    for k in (3, 1, 2, 0):
        total = None
        for side, (gate_ref, up_ref, _) in enumerate(weights):
            for matrix, grads in ((gate_ref, gates), (up_ref, ups)):
                term = lax.dot_general(
                    grads[:, side * HIDDEN : (side + 1) * HIDDEN],
                    matrix[pl.ds(starts[k], BLOCK), :],
                    transposed,
                    preferred_element_type=f32,
                )
                total = term if total is None else total + term
        out = outs[k]
        out[:total_rows, :] = total.astype(out.dtype)
        out[total_rows:, :] = jnp.zeros((TAIL, BLOCK), out.dtype)
        if k == 0:
            tail = jnp.where(row == 0, line, 0.0)
        else:
            tail = jnp.where(row == 0, high, jnp.where(row == 1, line - high, 0.0))
        out[total_rows:, :total_rows] = tail.astype(out.dtype)


def expert(place, groups, far, own_weights, other_weights):
    counts = tuple(group[0].shape[0] // (2 * PIECE) for group in groups)
    rows = sum(counts) * PIECE
    flat = [block for group in groups for block in group] + list(far)
    vmem = pl.BlockSpec(memory_space=pltpu.VMEM)
    out_shape = [
        jax.ShapeDtypeStruct((rows + TAIL, BLOCK), jnp.float32 if k == 0 else jnp.bfloat16)
        for k in range(4)
    ]
    features = 4 * BLOCK
    return pl.pallas_call(
        functools.partial(expert_body, counts),
        in_specs=[pl.BlockSpec(memory_space=pltpu.SMEM)] + [vmem] * (len(flat) + 6),
        out_specs=[vmem] * 4,
        out_shape=out_shape,
        scratch_shapes=[
            pltpu.VMEM((rows, features), jnp.bfloat16),
            pltpu.VMEM((rows, features), jnp.bfloat16),
            pltpu.VMEM((rows, 2 * HIDDEN), jnp.bfloat16),
            pltpu.VMEM((rows, 2 * HIDDEN), jnp.bfloat16),
        ],
        compiler_params=pltpu.CompilerParams(vmem_limit_bytes=8 * 1024 * 1024),
        cost_estimate=pl.CostEstimate(
            flops=20 * rows * features * HIDDEN,
            bytes_accessed=12 * features * HIDDEN,
            transcendentals=rows * HIDDEN * 2,
        ),
        name="expert",
    )(place, *flat, *own_weights, *other_weights)


SMALL = pltpu.CompilerParams(vmem_limit_bytes=4 * 1024 * 1024)
WIDE = BLOCK + 128
VMEM = pl.BlockSpec(memory_space=pltpu.VMEM)
SMEM = pl.BlockSpec(memory_space=pltpu.SMEM)


def as_column(line):
    square = (line.shape[1], line.shape[1])
    diagonal = lax.broadcasted_iota(jnp.int32, square, 0) == lax.broadcasted_iota(jnp.int32, square, 1)
    return jnp.sum(jnp.where(diagonal, line, jnp.zeros_like(line)), axis=1, keepdims=True)


def seats(spot_ref, quota_ref, choices, steps, half, slot):
    f32, bf16 = jnp.float32, jnp.bfloat16
    expert_of = ((spot_ref[1] + steps) & 3) * 2 + (half ^ spot_ref[2])
    quota = jnp.zeros_like(expert_of)
    for index in range(EXPERTS):
        quota = jnp.where(expert_of == index, quota_ref[0, index], quota)
    chosen = [as_column(choices[k : k + 1, :]) == expert_of for k in range(2)]
    taken = jnp.where(chosen[0], 1.0, jnp.where(chosen[1], 1.0, 0.0)).astype(bf16)
    tokens = choices.shape[1]
    square = (tokens, tokens)
    earlier = lax.broadcasted_iota(jnp.int32, square, 1) < lax.broadcasted_iota(jnp.int32, square, 0)
    before = jnp.dot(jnp.where(earlier, 1.0, 0.0).astype(bf16), taken, preferred_element_type=f32)
    seated = jnp.where(slot < quota, slot, -1).astype(f32) == before
    return [jnp.where(pick, jnp.where(seated, 1.0, 0.0), 0.0) for pick in chosen]


def front_body(spot_ref, quota_ref, choices_ref, x_hbm, d_hbm, *refs):
    outs, (x_ref, d_ref, arrivals) = refs[:4], refs[4:]
    copies = [
        pltpu.make_async_copy(x_hbm, x_ref, arrivals.at[0]),
        pltpu.make_async_copy(d_hbm, d_ref, arrivals.at[1]),
    ]
    for copy in copies:
        copy.start()
    lane = lax.broadcasted_iota(jnp.int32, (1, 192), 1)
    inner = lane % 24
    first, second = seats(
        spot_ref, quota_ref, choices_ref[...], lane // 48, (lane // 24) & 1, lane % CAP
    )
    hit = first + second
    tokens = (((0,), (0,)), ((), ()))
    for copy in copies:
        copy.wait()
    rows = lax.dot_general(
        jnp.where(inner < CAP, hit, 0.0).astype(jnp.bfloat16),
        x_ref[...],
        tokens,
        preferred_element_type=jnp.float32,
    ) + lax.dot_general(
        jnp.where(inner >= CAP, hit, 0.0).astype(jnp.bfloat16),
        d_ref[...],
        tokens,
        preferred_element_type=jnp.float32,
    )
    for step in range(4):
        outs[step][...] = rows[48 * step : 48 * step + 48].astype(jnp.bfloat16)


def front(spot, quota, choices, x, d):
    return pl.pallas_call(
        front_body,
        in_specs=[SMEM, SMEM, VMEM] + [pl.BlockSpec(memory_space=pltpu.HBM)] * 2,
        out_specs=[VMEM] * 4,
        out_shape=[jax.ShapeDtypeStruct((48, BLOCK), jnp.bfloat16)] * 4,
        scratch_shapes=[
            pltpu.VMEM(x.shape, x.dtype),
            pltpu.VMEM(d.shape, d.dtype),
            pltpu.SemaphoreType.DMA((2,)),
        ],
        compiler_params=SMALL,
        name="front",
    )(spot, quota, choices, x, d)


def hold_body(*refs):
    count = len(refs) // 2
    copies = [
        pltpu.make_async_copy(refs[at], refs[count + at], refs[-1].at[at]) for at in range(count)
    ]
    for copy in copies:
        copy.start()
    for copy in copies:
        copy.wait()


def hold(weights):
    return pl.pallas_call(
        hold_body,
        in_specs=[pl.BlockSpec(memory_space=pl.ANY)] * len(weights),
        out_specs=[VMEM] * len(weights),
        out_shape=[jax.ShapeDtypeStruct(w.shape, w.dtype) for w in weights],
        scratch_shapes=[pltpu.SemaphoreType.DMA((len(weights),))],
        compiler_params=SMALL,
        name="hold",
    )(*weights)


def sort_body(*refs):
    source = lax.broadcasted_iota(jnp.int32, (96, 48), 1)
    target = lax.broadcasted_iota(jnp.int32, (96, 48), 0)
    kind, slot = (source // CAP) & 1, source % CAP
    for half in range(2):
        total = 0.0
        for step in range(4):
            goal = kind * PIECE + step * CAP + slot
            pick = jnp.where(source // 24 == half, goal, -1) == target
            total = total + jnp.dot(
                jnp.where(pick, 1.0, 0.0).astype(jnp.bfloat16),
                refs[step][...],
                preferred_element_type=jnp.float32,
            )
        refs[4 + half][...] = total.astype(jnp.bfloat16)


def sort_rows(parts):
    return pl.pallas_call(
        sort_body,
        in_specs=[VMEM] * 4,
        out_specs=[VMEM] * 2,
        out_shape=[jax.ShapeDtypeStruct((96, BLOCK), jnp.bfloat16)] * 2,
        compiler_params=SMALL,
        name="sort_rows",
    )(*parts)


def tail_columns(product, rows):
    lane = lax.broadcasted_iota(jnp.int32, (rows, 128), 1)
    high = product.astype(jnp.bfloat16).astype(jnp.float32)
    return jnp.where(lane == 0, high, jnp.where(lane == 1, product - high, 0.0))


def collect_body(count, *refs):
    blocks, outs = refs[:count], refs[count:]
    rows = blocks[0].shape[0] - TAIL
    total = sum(block[...].astype(jnp.float32) for block in blocks)
    square = (rows, rows)
    diagonal = lax.broadcasted_iota(jnp.int32, square, 0) == lax.broadcasted_iota(jnp.int32, square, 1)
    line = total[rows : rows + 1, :rows] + total[rows + 1 : rows + 2, :rows]
    column = jnp.sum(jnp.where(diagonal, line, 0.0), axis=1, keepdims=True)
    tail = tail_columns(column, rows)
    for at, out in enumerate(outs):
        part = slice(at * PIECE, (at + 1) * PIECE)
        out[:, :BLOCK] = total[part].astype(out.dtype)
        out[:, BLOCK:] = tail[part].astype(out.dtype)


def collect(blocks, types):
    return pl.pallas_call(
        functools.partial(collect_body, len(blocks)),
        in_specs=[VMEM] * len(blocks),
        out_specs=[VMEM] * len(types),
        out_shape=[jax.ShapeDtypeStruct((PIECE, WIDE), t) for t in types],
        compiler_params=SMALL,
        name="collect",
    )(*blocks)


def homeward_body(*refs):
    f32, bf16 = jnp.float32, jnp.bfloat16
    rows = []
    for half in range(2):
        total = sum(refs[4 * half + at][...].astype(f32) for at in range(4))
        product = total[:, BLOCK : BLOCK + 1] + total[:, BLOCK + 1 : BLOCK + 2]
        rows.append((total[:, :BLOCK].astype(bf16), tail_columns(product, PIECE).astype(bf16)))
    source = lax.broadcasted_iota(jnp.int32, (32, PIECE), 1)
    target = lax.broadcasted_iota(jnp.int32, (32, PIECE), 0)
    for step in range(4):
        out = refs[8 + step]
        picks = [
            jnp.where(
                jnp.where(source // CAP == step, half * CAP + source % CAP, -1) == target, 1.0, 0.0
            ).astype(bf16)
            for half in range(2)
        ]
        for part, lanes in ((0, slice(0, BLOCK)), (1, slice(BLOCK, WIDE))):
            out[:, lanes] = sum(
                jnp.dot(picks[half], rows[half][part], preferred_element_type=f32) for half in range(2)
            ).astype(bf16)


def homeward(parts):
    return pl.pallas_call(
        homeward_body,
        in_specs=[VMEM] * 8,
        out_specs=[VMEM] * 4,
        out_shape=[jax.ShapeDtypeStruct((32, WIDE), jnp.bfloat16)] * 4,
        compiler_params=SMALL,
        name="homeward",
    )(*parts)


def finish_body(spot_ref, quota_ref, choices_ref, mixing_ref, *refs):
    f32, bf16 = jnp.float32, jnp.bfloat16
    parts, (token_ref, gate_ref) = refs[:4], refs[4:]
    lane = lax.broadcasted_iota(jnp.int32, (1, 128), 1)
    inner = lane & 31
    half = jnp.where(inner < CAP, 0, 1)
    slot = jnp.where(inner < 2 * CAP, inner - half * CAP, 1 << 20)
    picks = seats(spot_ref, quota_ref, choices_ref[...], lane >> 5, half, slot)
    weight = sum(picks[k] * as_column(mixing_ref[k : k + 1, :]) for k in range(2))
    total = 0.0
    tails = jnp.concatenate([part[:, BLOCK:] for part in parts], axis=0)
    rows = jnp.concatenate([part[:, :BLOCK] for part in parts], axis=0)
    for _ in range(3):
        piece = weight.astype(bf16)
        weight = weight - piece.astype(f32)
        total = total + jnp.dot(piece, rows, preferred_element_type=f32)
    token_ref[...] = total.astype(bf16)
    for k in range(2):
        found = lax.dot_general(
            tails, picks[k].astype(bf16), (((0,), (1,)), ((), ())), preferred_element_type=f32
        )
        gate_ref[k : k + 1, :] = found[0:1, :] + found[1:2, :]


def finish(spot, quota, choices, mixing, parts):
    return pl.pallas_call(
        finish_body,
        in_specs=[SMEM, SMEM] + [VMEM] * 6,
        out_specs=[VMEM] * 2,
        out_shape=[
            jax.ShapeDtypeStruct((128, BLOCK), jnp.bfloat16),
            jax.ShapeDtypeStruct((2, 128), jnp.float32),
        ],
        compiler_params=SMALL,
        name="finish",
    )(spot, quota, choices, mixing, *parts)


def local(
    layer_activations_input,
    output_gradient,
    specialist_choices_matrix,
    mixing_coefficients,
    quota_table,
    gating_matrix,
    widening_matrix,
    contracting_matrix,
):
    f32, bf16 = jnp.float32, jnp.bfloat16
    barrier = lax.optimization_barrier
    own = lax.axis_index("ed").astype(jnp.int32)
    spot = jnp.stack([lax.axis_index("tp").astype(jnp.int32), own >> 4, (own >> 3) & 1])
    own_weights = (gating_matrix, widening_matrix, contracting_matrix)
    gating, widening, spot = barrier((gating_matrix, widening_matrix, spot))
    other_gate, other_up = across_cores(gating), across_cores(widening)

    choices = specialist_choices_matrix.T
    payload = front(spot, quota_table, choices, layer_activations_input, output_gradient)
    arrived = [payload[0]] + [along_y(payload[step], step) for step in (1, 2, 3)]
    *arrived, other_gate, other_up, contracting = barrier(
        (*arrived, other_gate, other_up, contracting_matrix)
    )
    other_down = across_cores(contracting)
    same, other = sort_rows(arrived)

    def opposite(left, right):
        middle = left.shape[0] // 2
        return along_x(left[:middle], 1), along_x(right[middle:], -1)

    near = [same, along_z(same, 1), along_z(other, 4), along_z(other, 5)]
    distant = [along_z(same, 2), along_z(same, 3), along_z(other, 6), along_z(other, 7)]
    block1 = jnp.concatenate(near, axis=0)
    block1, other_down, *held = barrier((block1, other_down, *hold(own_weights[1:])))
    own_weights = (gating_matrix, *held)
    left1, right1 = along_x(block1, 1), along_x(block1, -1)
    block2 = jnp.concatenate(distant, axis=0)
    block2, left1, right1 = barrier((block2, left1, right1))
    left2, right2 = along_x(block2, 1), along_x(block2, -1)
    groups1, far1 = [(block1, left1, right1)], opposite(left1, right1)
    other_weights = (other_gate, other_up, other_down)
    first = expert(spot, groups1, far1, own_weights, other_weights)
    mine, to_left, to_right, to_far = first
    middle = 2 * PIECE
    passing = [along_x(to_far[:middle], 1), along_x(to_far[middle:], -1)]
    left2, right2, mine, to_left, to_right = barrier((left2, right2, mine, to_left, to_right))
    far2 = opposite(left2, right2)
    low = (to_right[:middle].astype(f32) + passing[0].astype(f32)).astype(bf16)
    high = (to_left[middle:].astype(f32) + passing[1].astype(f32)).astype(bf16)
    to_right = jnp.concatenate([low, to_right[middle:]], axis=0)
    to_left = jnp.concatenate([to_left[:middle], high], axis=0)
    *far2, to_right, to_left = barrier((*far2, to_right, to_left))
    second = expert(spot, [(block2, left2, right2)], far2, own_weights, other_weights)

    back1 = collect((mine, along_x(to_left, -1), along_x(to_right, 1)), (f32, bf16, bf16, bf16))
    back1 = [back1[0]] + [along_z(part, flip) for part, flip in zip(back1[1:], (1, 4, 5))]
    mine, to_left, to_right, to_far = second
    back2 = collect(
        (mine, along_x(to_far, 2), along_x(to_left, -1), along_x(to_right, 1)), (bf16,) * 4
    )
    back2 = [along_z(part, flip) for part, flip in zip(back2, (2, 3, 6, 7))]
    same_rows = (back1[0], back1[1], back2[0], back2[1])
    other_rows = (back1[2], back1[3], back2[2], back2[3])
    returned = homeward((*same_rows, *other_rows))
    home = [returned[0]] + [along_y(returned[step], -step) for step in (1, 2, 3)]
    token_grads, gate_grads = finish(spot, quota_table, choices, mixing_coefficients.T, home)
    return token_grads, gate_grads.T


def solution(mesh):
    in_specs = (
        P("ed", "tp"),
        P("ed", "tp"),
        P("ed", None),
        P("ed", None),
        P("ed", None),
        P(None, ("ed", "tp")),
        P(None, ("ed", "tp")),
        P(("ed", "tp"), None),
    )
    out_specs = (P("ed", "tp"), P("ed", None))
    return jax.shard_map(local, mesh=mesh, in_specs=in_specs, out_specs=out_specs, check_vma=False)
```

```python
import functools

import jax
import jax.numpy as jnp
from jax import lax
from jax.experimental import pallas as pl
from jax.experimental.pallas import tpu as pltpu
from jax.sharding import PartitionSpec as P

EXPERTS = 8
CAP = 12
BLOCK = 768
HIDDEN = 512
CHUNK = 256
PIECE = 4 * CAP
TAIL = 16
OFFSETS = (0, 3, 1, 2)


def along_x(value, step):
    return lax.ppermute(value, "tp", [(i, (i + step) % 4) for i in range(4)])


def along_y(value, step):
    return lax.ppermute(value, "ed", [(i, (i + 16 * step) % 64) for i in range(64)])


def along_z(value, flip):
    return lax.ppermute(value, "ed", [(i, i ^ (flip * 2)) for i in range(64)])


def across_cores(value):
    return lax.ppermute(value, "ed", [(i, i ^ 1) for i in range(64)])


def expert_body(counts, place_ref, *refs):
    groups = len(counts)
    group_refs = refs[: 3 * groups]
    far_low, far_high = refs[3 * groups : 3 * groups + 2]
    refs = refs[3 * groups + 2 :]
    outs = refs[6:10]
    xs, ys, gates, ups = refs[10:]
    weights = (refs[:3], refs[3:6])
    f32, bf16 = jnp.float32, jnp.bfloat16
    total_rows = sum(counts) * PIECE
    place = place_ref[0]
    starts = [pl.multiple_of(((place + off) % 4) * BLOCK, BLOCK) for off in OFFSETS]
    base = 0
    for at, count in enumerate(counts):
        own, left, right = group_refs[3 * at : 3 * at + 3]
        half = count * PIECE
        origin = base
        for piece in range(count):
            for kind, goal in enumerate((xs, ys)):
                line = (2 * piece + kind) * PIECE
                rows = slice(base, base + PIECE)
                for k, block in enumerate((own, left, right)):
                    goal[rows, pl.ds(starts[k], BLOCK)] = block[line : line + PIECE, :]
                far = far_low if line < half else far_high
                from_row = origin + line % half
                goal[rows, pl.ds(starts[3], BLOCK)] = far[from_row : from_row + PIECE, :]
            base += PIECE
    transposed = (((1,), (1,)), ((), ()))
    dots = jnp.zeros((total_rows, 128), f32)
    for side, (gate_ref, up_ref, down_ref) in enumerate(weights):
        for chunk in range(HIDDEN // CHUNK):
            columns = slice(chunk * CHUNK, (chunk + 1) * CHUNK)
            pre_gate = jnp.dot(xs[...], gate_ref[:, columns], preferred_element_type=f32)
            pre_up = jnp.dot(xs[...], up_ref[:, columns], preferred_element_type=f32)
            back_act = lax.dot_general(
                ys[...], down_ref[columns, :], transposed, preferred_element_type=f32
            )
            sigmoid_gate = jax.nn.sigmoid(pre_gate)
            swish = pre_gate * sigmoid_gate
            activation = (swish * pre_up).astype(bf16)
            product = activation.astype(f32) * back_act
            for lane in range(CHUNK // 128):
                dots = dots + product[:, lane * 128 : (lane + 1) * 128]
            at = slice(side * HIDDEN + chunk * CHUNK, side * HIDDEN + (chunk + 1) * CHUNK)
            gates[:, at] = (
                back_act * pre_up * sigmoid_gate * (1.0 + pre_gate * (1.0 - sigmoid_gate))
            ).astype(bf16)
            ups[:, at] = (back_act * swish).astype(bf16)
    square = (total_rows, total_rows)
    diagonal = lax.broadcasted_iota(jnp.int32, square, 0) == lax.broadcasted_iota(jnp.int32, square, 1)
    column = jnp.sum(dots, axis=1, keepdims=True)
    line = jnp.sum(jnp.where(diagonal, column, 0.0), axis=0, keepdims=True)
    line = jnp.broadcast_to(line, (TAIL, total_rows))
    row = lax.broadcasted_iota(jnp.int32, line.shape, 0)
    high = line.astype(bf16).astype(f32)
    for k in (3, 1, 2, 0):
        total = None
        for side, (gate_ref, up_ref, _) in enumerate(weights):
            for matrix, grads in ((gate_ref, gates), (up_ref, ups)):
                term = lax.dot_general(
                    grads[:, side * HIDDEN : (side + 1) * HIDDEN],
                    matrix[pl.ds(starts[k], BLOCK), :],
                    transposed,
                    preferred_element_type=f32,
                )
                total = term if total is None else total + term
        out = outs[k]
        out[:total_rows, :] = total.astype(out.dtype)
        out[total_rows:, :] = jnp.zeros((TAIL, BLOCK), out.dtype)
        if k == 0:
            tail = jnp.where(row == 0, line, 0.0)
        else:
            tail = jnp.where(row == 0, high, jnp.where(row == 1, line - high, 0.0))
        out[total_rows:, :total_rows] = tail.astype(out.dtype)


def expert(place, groups, far, own_weights, other_weights):
    counts = tuple(group[0].shape[0] // (2 * PIECE) for group in groups)
    rows = sum(counts) * PIECE
    flat = [block for group in groups for block in group] + list(far)
    vmem = pl.BlockSpec(memory_space=pltpu.VMEM)
    out_shape = [
        jax.ShapeDtypeStruct((rows + TAIL, BLOCK), jnp.float32 if k == 0 else jnp.bfloat16)
        for k in range(4)
    ]
    features = 4 * BLOCK
    return pl.pallas_call(
        functools.partial(expert_body, counts),
        in_specs=[pl.BlockSpec(memory_space=pltpu.SMEM)] + [vmem] * (len(flat) + 6),
        out_specs=[vmem] * 4,
        out_shape=out_shape,
        scratch_shapes=[
            pltpu.VMEM((rows, features), jnp.bfloat16),
            pltpu.VMEM((rows, features), jnp.bfloat16),
            pltpu.VMEM((rows, 2 * HIDDEN), jnp.bfloat16),
            pltpu.VMEM((rows, 2 * HIDDEN), jnp.bfloat16),
        ],
        compiler_params=pltpu.CompilerParams(vmem_limit_bytes=8 * 1024 * 1024),
        cost_estimate=pl.CostEstimate(
            flops=20 * rows * features * HIDDEN,
            bytes_accessed=12 * features * HIDDEN,
            transcendentals=rows * HIDDEN * 2,
        ),
        name="expert",
    )(place, *flat, *own_weights, *other_weights)


SMALL = pltpu.CompilerParams(vmem_limit_bytes=4 * 1024 * 1024)
WIDE = BLOCK + 128
VMEM = pl.BlockSpec(memory_space=pltpu.VMEM)
SMEM = pl.BlockSpec(memory_space=pltpu.SMEM)


def as_column(line):
    square = (line.shape[1], line.shape[1])
    diagonal = lax.broadcasted_iota(jnp.int32, square, 0) == lax.broadcasted_iota(jnp.int32, square, 1)
    return jnp.sum(jnp.where(diagonal, line, jnp.zeros_like(line)), axis=1, keepdims=True)


def seats(spot_ref, quota_ref, choices, steps, half, slot):
    f32, bf16 = jnp.float32, jnp.bfloat16
    expert_of = ((spot_ref[1] + steps) & 3) * 2 + (half ^ spot_ref[2])
    quota = jnp.zeros_like(expert_of)
    limits = quota_ref[...]
    for index in range(EXPERTS):
        quota = jnp.where(expert_of == index, limits[:, index : index + 1], quota)
    chosen = [as_column(choices[k : k + 1, :]) == expert_of for k in range(2)]
    taken = jnp.where(chosen[0], 1.0, jnp.where(chosen[1], 1.0, 0.0)).astype(bf16)
    tokens = choices.shape[1]
    square = (tokens, tokens)
    earlier = lax.broadcasted_iota(jnp.int32, square, 1) < lax.broadcasted_iota(jnp.int32, square, 0)
    before = jnp.dot(jnp.where(earlier, 1.0, 0.0).astype(bf16), taken, preferred_element_type=f32)
    seated = jnp.where(slot < quota, slot, -1).astype(f32) == before
    return [jnp.where(pick, jnp.where(seated, 1.0, 0.0), 0.0) for pick in chosen]


def front_body(spot_ref, quota_ref, choices_ref, x_ref, d_ref, *outs):
    lane = lax.broadcasted_iota(jnp.int32, (1, 192), 1)
    inner = lane % 24
    first, second = seats(
        spot_ref, quota_ref, choices_ref[...], lane // 48, (lane // 24) & 1, lane % CAP
    )
    hit = first + second
    tokens = (((0,), (0,)), ((), ()))
    rows = lax.dot_general(
        jnp.where(inner < CAP, hit, 0.0).astype(jnp.bfloat16),
        x_ref[...],
        tokens,
        preferred_element_type=jnp.float32,
    ) + lax.dot_general(
        jnp.where(inner >= CAP, hit, 0.0).astype(jnp.bfloat16),
        d_ref[...],
        tokens,
        preferred_element_type=jnp.float32,
    )
    for step in range(4):
        outs[step][...] = rows[48 * step : 48 * step + 48].astype(jnp.bfloat16)


def front(spot, quota, choices, x, d):
    whole = lambda array: pl.BlockSpec(array.shape, lambda step: (0, 0))
    out = jax.ShapeDtypeStruct((48, BLOCK), jnp.bfloat16)
    return pl.pallas_call(
        front_body,
        grid=(1,),
        in_specs=[SMEM, whole(quota), whole(choices), whole(x), whole(d)],
        out_specs=[whole(out)] * 4,
        out_shape=[out] * 4,
        compiler_params=pltpu.CompilerParams(vmem_limit_bytes=57 * 1024 * 1024),
        name="front",
    )(spot, quota, choices, x, d)


def hold_body(*refs):
    count = len(refs) // 2
    copies = [
        pltpu.make_async_copy(refs[at], refs[count + at], refs[-1].at[at]) for at in range(count)
    ]
    for copy in copies:
        copy.start()
    for copy in copies:
        copy.wait()


def hold(weights):
    return pl.pallas_call(
        hold_body,
        in_specs=[pl.BlockSpec(memory_space=pl.ANY)] * len(weights),
        out_specs=[VMEM] * len(weights),
        out_shape=[jax.ShapeDtypeStruct(w.shape, w.dtype) for w in weights],
        scratch_shapes=[pltpu.SemaphoreType.DMA((len(weights),))],
        compiler_params=SMALL,
        name="hold",
    )(*weights)


def sort_body(*refs):
    source = lax.broadcasted_iota(jnp.int32, (96, 48), 1)
    target = lax.broadcasted_iota(jnp.int32, (96, 48), 0)
    kind, slot = (source // CAP) & 1, source % CAP
    for half in range(2):
        total = 0.0
        for step in range(4):
            goal = kind * PIECE + step * CAP + slot
            pick = jnp.where(source // 24 == half, goal, -1) == target
            total = total + jnp.dot(
                jnp.where(pick, 1.0, 0.0).astype(jnp.bfloat16),
                refs[step][...],
                preferred_element_type=jnp.float32,
            )
        refs[4 + half][...] = total.astype(jnp.bfloat16)


def sort_rows(parts):
    return pl.pallas_call(
        sort_body,
        in_specs=[VMEM] * 4,
        out_specs=[VMEM] * 2,
        out_shape=[jax.ShapeDtypeStruct((96, BLOCK), jnp.bfloat16)] * 2,
        compiler_params=SMALL,
        name="sort_rows",
    )(*parts)


def tail_columns(product, rows):
    lane = lax.broadcasted_iota(jnp.int32, (rows, 128), 1)
    high = product.astype(jnp.bfloat16).astype(jnp.float32)
    return jnp.where(lane == 0, high, jnp.where(lane == 1, product - high, 0.0))


def collect_body(count, *refs):
    blocks, outs = refs[:count], refs[count:]
    rows = blocks[0].shape[0] - TAIL
    total = sum(block[...].astype(jnp.float32) for block in blocks)
    square = (rows, rows)
    diagonal = lax.broadcasted_iota(jnp.int32, square, 0) == lax.broadcasted_iota(jnp.int32, square, 1)
    line = total[rows : rows + 1, :rows] + total[rows + 1 : rows + 2, :rows]
    column = jnp.sum(jnp.where(diagonal, line, 0.0), axis=1, keepdims=True)
    tail = tail_columns(column, rows)
    for at, out in enumerate(outs):
        part = slice(at * PIECE, (at + 1) * PIECE)
        out[:, :BLOCK] = total[part].astype(out.dtype)
        out[:, BLOCK:] = tail[part].astype(out.dtype)


def collect(blocks, types):
    return pl.pallas_call(
        functools.partial(collect_body, len(blocks)),
        in_specs=[VMEM] * len(blocks),
        out_specs=[VMEM] * len(types),
        out_shape=[jax.ShapeDtypeStruct((PIECE, WIDE), t) for t in types],
        compiler_params=SMALL,
        name="collect",
    )(*blocks)


def homeward_body(*refs):
    f32, bf16 = jnp.float32, jnp.bfloat16
    rows = []
    for half in range(2):
        total = sum(refs[4 * half + at][...].astype(f32) for at in range(4))
        product = total[:, BLOCK : BLOCK + 1] + total[:, BLOCK + 1 : BLOCK + 2]
        rows.append((total[:, :BLOCK].astype(bf16), tail_columns(product, PIECE).astype(bf16)))
    source = lax.broadcasted_iota(jnp.int32, (32, PIECE), 1)
    target = lax.broadcasted_iota(jnp.int32, (32, PIECE), 0)
    for step in range(4):
        out = refs[8 + step]
        picks = [
            jnp.where(
                jnp.where(source // CAP == step, half * CAP + source % CAP, -1) == target, 1.0, 0.0
            ).astype(bf16)
            for half in range(2)
        ]
        for part, lanes in ((0, slice(0, BLOCK)), (1, slice(BLOCK, WIDE))):
            out[:, lanes] = sum(
                jnp.dot(picks[half], rows[half][part], preferred_element_type=f32) for half in range(2)
            ).astype(bf16)


def homeward(parts):
    return pl.pallas_call(
        homeward_body,
        in_specs=[VMEM] * 8,
        out_specs=[VMEM] * 4,
        out_shape=[jax.ShapeDtypeStruct((32, WIDE), jnp.bfloat16)] * 4,
        compiler_params=SMALL,
        name="homeward",
    )(*parts)


def finish_body(spot_ref, quota_ref, choices_ref, mixing_ref, *refs):
    f32, bf16 = jnp.float32, jnp.bfloat16
    parts, (token_ref, gate_ref) = refs[:4], refs[4:]
    lane = lax.broadcasted_iota(jnp.int32, (1, 128), 1)
    inner = lane & 31
    half = jnp.where(inner < CAP, 0, 1)
    slot = jnp.where(inner < 2 * CAP, inner - half * CAP, 1 << 20)
    picks = seats(spot_ref, quota_ref, choices_ref[...], lane >> 5, half, slot)
    weight = sum(picks[k] * as_column(mixing_ref[k : k + 1, :]) for k in range(2))
    total = 0.0
    tails = jnp.concatenate([part[:, BLOCK:] for part in parts], axis=0)
    rows = jnp.concatenate([part[:, :BLOCK] for part in parts], axis=0)
    for _ in range(3):
        piece = weight.astype(bf16)
        weight = weight - piece.astype(f32)
        total = total + jnp.dot(piece, rows, preferred_element_type=f32)
    token_ref[...] = total.astype(bf16)
    for k in range(2):
        found = lax.dot_general(
            tails, picks[k].astype(bf16), (((0,), (1,)), ((), ())), preferred_element_type=f32
        )
        gate_ref[k : k + 1, :] = found[0:1, :] + found[1:2, :]


def finish(spot, quota, choices, mixing, parts):
    return pl.pallas_call(
        finish_body,
        in_specs=[SMEM] + [VMEM] * 7,
        out_specs=[VMEM] * 2,
        out_shape=[
            jax.ShapeDtypeStruct((128, BLOCK), jnp.bfloat16),
            jax.ShapeDtypeStruct((2, 128), jnp.float32),
        ],
        compiler_params=SMALL,
        name="finish",
    )(spot, quota, choices, mixing, *parts)


def local(
    layer_activations_input,
    output_gradient,
    specialist_choices_matrix,
    mixing_coefficients,
    quota_table,
    gating_matrix,
    widening_matrix,
    contracting_matrix,
):
    f32, bf16 = jnp.float32, jnp.bfloat16
    barrier = lax.optimization_barrier
    own = lax.axis_index("ed").astype(jnp.int32)
    spot = jnp.stack([lax.axis_index("tp").astype(jnp.int32), own >> 4, (own >> 3) & 1])
    own_weights = (gating_matrix, widening_matrix, contracting_matrix)
    gating, widening, spot = barrier((gating_matrix, widening_matrix, spot))
    other_gate, other_up = across_cores(gating), across_cores(widening)

    choices = specialist_choices_matrix.T
    payload = front(spot, quota_table, choices, layer_activations_input, output_gradient)
    arrived = [payload[0]] + [along_y(payload[step], step) for step in (1, 2, 3)]
    *arrived, other_gate, other_up, contracting = barrier(
        (*arrived, other_gate, other_up, contracting_matrix)
    )
    other_down = across_cores(contracting)
    same, other = sort_rows(arrived)

    def opposite(left, right):
        middle = left.shape[0] // 2
        return along_x(left[:middle], 1), along_x(right[middle:], -1)

    near = [same, along_z(same, 1), along_z(other, 4), along_z(other, 5)]
    distant = [along_z(same, 2), along_z(same, 3), along_z(other, 6), along_z(other, 7)]
    block1 = jnp.concatenate(near, axis=0)
    block1, other_down, *held = barrier((block1, other_down, *hold(own_weights[1:])))
    own_weights = (gating_matrix, *held)
    left1, right1 = along_x(block1, 1), along_x(block1, -1)
    block2 = jnp.concatenate(distant, axis=0)
    block2, left1, right1 = barrier((block2, left1, right1))
    left2, right2 = along_x(block2, 1), along_x(block2, -1)
    groups1, far1 = [(block1, left1, right1)], opposite(left1, right1)
    other_weights = (other_gate, other_up, other_down)
    first = expert(spot, groups1, far1, own_weights, other_weights)
    mine, to_left, to_right, to_far = first
    middle = 2 * PIECE
    passing = [along_x(to_far[:middle], 1), along_x(to_far[middle:], -1)]
    left2, right2, mine, to_left, to_right = barrier((left2, right2, mine, to_left, to_right))
    far2 = opposite(left2, right2)
    low = (to_right[:middle].astype(f32) + passing[0].astype(f32)).astype(bf16)
    high = (to_left[middle:].astype(f32) + passing[1].astype(f32)).astype(bf16)
    to_right = jnp.concatenate([low, to_right[middle:]], axis=0)
    to_left = jnp.concatenate([to_left[:middle], high], axis=0)
    *far2, to_right, to_left = barrier((*far2, to_right, to_left))
    second = expert(spot, [(block2, left2, right2)], far2, own_weights, other_weights)

    back1 = collect((mine, along_x(to_left, -1), along_x(to_right, 1)), (f32, bf16, bf16, bf16))
    back1 = [back1[0]] + [along_z(part, flip) for part, flip in zip(back1[1:], (1, 4, 5))]
    mine, to_left, to_right, to_far = second
    back2 = collect(
        (mine, along_x(to_far, 2), along_x(to_left, -1), along_x(to_right, 1)), (bf16,) * 4
    )
    back2 = [along_z(part, flip) for part, flip in zip(back2, (2, 3, 6, 7))]
    same_rows = (back1[0], back1[1], back2[0], back2[1])
    other_rows = (back1[2], back1[3], back2[2], back2[3])
    returned = homeward((*same_rows, *other_rows))
    home = [returned[0]] + [along_y(returned[step], -step) for step in (1, 2, 3)]
    token_grads, gate_grads = finish(spot, quota_table, choices, mixing_coefficients.T, home)
    return token_grads, gate_grads.T


def solution(mesh):
    in_specs = (
        P("ed", "tp"),
        P("ed", "tp"),
        P("ed", None),
        P("ed", None),
        P("ed", None),
        P(None, ("ed", "tp")),
        P(None, ("ed", "tp")),
        P(("ed", "tp"), None),
    )
    out_specs = (P("ed", "tp"), P("ed", None))
    return jax.shard_map(local, mesh=mesh, in_specs=in_specs, out_specs=out_specs, check_vma=False)
```

```python
import functools

import jax
import jax.numpy as jnp
from jax import lax
from jax.experimental import pallas as pl
from jax.experimental.pallas import tpu as pltpu
from jax.sharding import PartitionSpec as P

EXPERTS = 8
CAP = 12
BLOCK = 768
HIDDEN = 512
CHUNK = 256
PIECE = 4 * CAP
TAIL = 16
OFFSETS = (0, 3, 1, 2)


def along_x(value, step):
    return lax.ppermute(value, "tp", [(i, (i + step) % 4) for i in range(4)])


def along_y(value, step):
    return lax.ppermute(value, "ed", [(i, (i + 16 * step) % 64) for i in range(64)])


def along_z(value, flip):
    return lax.ppermute(value, "ed", [(i, i ^ (flip * 2)) for i in range(64)])


def across_cores(value):
    return lax.ppermute(value, "ed", [(i, i ^ 1) for i in range(64)])


def expert_body(counts, place_ref, *refs):
    groups = len(counts)
    group_refs = refs[: 3 * groups]
    far_low, far_high = refs[3 * groups : 3 * groups + 2]
    refs = refs[3 * groups + 2 :]
    outs = refs[6:10]
    xs, ys, gates, ups = refs[10:]
    weights = (refs[:3], refs[3:6])
    f32, bf16 = jnp.float32, jnp.bfloat16
    total_rows = sum(counts) * PIECE
    place = place_ref[0]
    starts = [pl.multiple_of(((place + off) % 4) * BLOCK, BLOCK) for off in OFFSETS]
    base = 0
    for at, count in enumerate(counts):
        own, left, right = group_refs[3 * at : 3 * at + 3]
        half = count * PIECE
        origin = base
        for piece in range(count):
            for kind, goal in enumerate((xs, ys)):
                line = (2 * piece + kind) * PIECE
                rows = slice(base, base + PIECE)
                for k, block in enumerate((own, left, right)):
                    goal[rows, pl.ds(starts[k], BLOCK)] = block[line : line + PIECE, :]
                far = far_low if line < half else far_high
                from_row = origin + line % half
                goal[rows, pl.ds(starts[3], BLOCK)] = far[from_row : from_row + PIECE, :]
            base += PIECE
    transposed = (((1,), (1,)), ((), ()))
    dots = jnp.zeros((total_rows, 128), f32)
    for side, (gate_ref, up_ref, down_ref) in enumerate(weights):
        for chunk in range(HIDDEN // CHUNK):
            columns = slice(chunk * CHUNK, (chunk + 1) * CHUNK)
            pre_gate = jnp.dot(xs[...], gate_ref[:, columns], preferred_element_type=f32)
            pre_up = jnp.dot(xs[...], up_ref[:, columns], preferred_element_type=f32)
            back_act = lax.dot_general(
                ys[...], down_ref[columns, :], transposed, preferred_element_type=f32
            )
            sigmoid_gate = jax.nn.sigmoid(pre_gate)
            swish = pre_gate * sigmoid_gate
            activation = (swish * pre_up).astype(bf16)
            product = activation.astype(f32) * back_act
            for lane in range(CHUNK // 128):
                dots = dots + product[:, lane * 128 : (lane + 1) * 128]
            at = slice(side * HIDDEN + chunk * CHUNK, side * HIDDEN + (chunk + 1) * CHUNK)
            gates[:, at] = (
                back_act * pre_up * sigmoid_gate * (1.0 + pre_gate * (1.0 - sigmoid_gate))
            ).astype(bf16)
            ups[:, at] = (back_act * swish).astype(bf16)
    square = (total_rows, total_rows)
    diagonal = lax.broadcasted_iota(jnp.int32, square, 0) == lax.broadcasted_iota(jnp.int32, square, 1)
    column = jnp.sum(dots, axis=1, keepdims=True)
    line = jnp.sum(jnp.where(diagonal, column, 0.0), axis=0, keepdims=True)
    line = jnp.broadcast_to(line, (TAIL, total_rows))
    row = lax.broadcasted_iota(jnp.int32, line.shape, 0)
    high = line.astype(bf16).astype(f32)
    for k in (3, 1, 2, 0):
        total = None
        for side, (gate_ref, up_ref, _) in enumerate(weights):
            for matrix, grads in ((gate_ref, gates), (up_ref, ups)):
                term = lax.dot_general(
                    grads[:, side * HIDDEN : (side + 1) * HIDDEN],
                    matrix[pl.ds(starts[k], BLOCK), :],
                    transposed,
                    preferred_element_type=f32,
                )
                total = term if total is None else total + term
        out = outs[k]
        out[:total_rows, :] = total.astype(out.dtype)
        out[total_rows:, :] = jnp.zeros((TAIL, BLOCK), out.dtype)
        if k == 0:
            tail = jnp.where(row == 0, line, 0.0)
        else:
            tail = jnp.where(row == 0, high, jnp.where(row == 1, line - high, 0.0))
        out[total_rows:, :total_rows] = tail.astype(out.dtype)


def expert(place, groups, far, own_weights, other_weights):
    counts = tuple(group[0].shape[0] // (2 * PIECE) for group in groups)
    rows = sum(counts) * PIECE
    flat = [block for group in groups for block in group] + list(far)
    vmem = pl.BlockSpec(memory_space=pltpu.VMEM)
    out_shape = [
        jax.ShapeDtypeStruct((rows + TAIL, BLOCK), jnp.float32 if k == 0 else jnp.bfloat16)
        for k in range(4)
    ]
    features = 4 * BLOCK
    return pl.pallas_call(
        functools.partial(expert_body, counts),
        in_specs=[pl.BlockSpec(memory_space=pltpu.SMEM)] + [vmem] * (len(flat) + 6),
        out_specs=[vmem] * 4,
        out_shape=out_shape,
        scratch_shapes=[
            pltpu.VMEM((rows, features), jnp.bfloat16),
            pltpu.VMEM((rows, features), jnp.bfloat16),
            pltpu.VMEM((rows, 2 * HIDDEN), jnp.bfloat16),
            pltpu.VMEM((rows, 2 * HIDDEN), jnp.bfloat16),
        ],
        compiler_params=pltpu.CompilerParams(vmem_limit_bytes=8 * 1024 * 1024),
        cost_estimate=pl.CostEstimate(
            flops=20 * rows * features * HIDDEN,
            bytes_accessed=12 * features * HIDDEN,
            transcendentals=rows * HIDDEN * 2,
        ),
        name="expert",
    )(place, *flat, *own_weights, *other_weights)


SMALL = pltpu.CompilerParams(vmem_limit_bytes=4 * 1024 * 1024)
WIDE = BLOCK + 128
VMEM = pl.BlockSpec(memory_space=pltpu.VMEM)
SMEM = pl.BlockSpec(memory_space=pltpu.SMEM)


def as_column(line):
    square = (line.shape[1], line.shape[1])
    diagonal = lax.broadcasted_iota(jnp.int32, square, 0) == lax.broadcasted_iota(jnp.int32, square, 1)
    return jnp.sum(jnp.where(diagonal, line, jnp.zeros_like(line)), axis=1, keepdims=True)


def seats(spot_ref, quota_ref, choices, steps, half, slot):
    f32, bf16 = jnp.float32, jnp.bfloat16
    expert_of = ((spot_ref[1] + steps) & 3) * 2 + (half ^ spot_ref[2])
    quota = jnp.zeros_like(expert_of)
    limits = quota_ref[...]
    for index in range(EXPERTS):
        quota = jnp.where(expert_of == index, limits[:, index : index + 1], quota)
    chosen = [as_column(choices[k : k + 1, :]) == expert_of for k in range(2)]
    taken = jnp.where(chosen[0], 1.0, jnp.where(chosen[1], 1.0, 0.0)).astype(bf16)
    tokens = choices.shape[1]
    square = (tokens, tokens)
    earlier = lax.broadcasted_iota(jnp.int32, square, 1) < lax.broadcasted_iota(jnp.int32, square, 0)
    before = jnp.dot(jnp.where(earlier, 1.0, 0.0).astype(bf16), taken, preferred_element_type=f32)
    seated = jnp.where(slot < quota, slot, -1).astype(f32) == before
    return [jnp.where(pick, jnp.where(seated, 1.0, 0.0), 0.0) for pick in chosen]


def front_body(spot_ref, quota_ref, choices_ref, x_ref, d_ref, *outs):
    lane = lax.broadcasted_iota(jnp.int32, (1, 192), 1)
    inner = lane % 24
    first, second = seats(
        spot_ref, quota_ref, choices_ref[...], lane // 48, (lane // 24) & 1, lane % CAP
    )
    hit = first + second
    tokens = (((0,), (0,)), ((), ()))
    rows = lax.dot_general(
        jnp.where(inner < CAP, hit, 0.0).astype(jnp.bfloat16),
        x_ref[...],
        tokens,
        preferred_element_type=jnp.float32,
    ) + lax.dot_general(
        jnp.where(inner >= CAP, hit, 0.0).astype(jnp.bfloat16),
        d_ref[...],
        tokens,
        preferred_element_type=jnp.float32,
    )
    for step in range(4):
        outs[step][...] = rows[48 * step : 48 * step + 48].astype(jnp.bfloat16)


def front(spot, quota, choices, x, d):
    whole = lambda array: pl.BlockSpec(array.shape, lambda step: (0, 0))
    out = jax.ShapeDtypeStruct((48, BLOCK), jnp.bfloat16)
    return pl.pallas_call(
        front_body,
        grid=(1,),
        in_specs=[SMEM, whole(quota), whole(choices), whole(x), whole(d)],
        out_specs=[whole(out)] * 4,
        out_shape=[out] * 4,
        compiler_params=pltpu.CompilerParams(vmem_limit_bytes=57 * 1024 * 1024),
        name="front",
    )(spot, quota, choices, x, d)


def hold_body(*refs):
    count = len(refs) // 2
    copies = [
        pltpu.make_async_copy(refs[at], refs[count + at], refs[-1].at[at]) for at in range(count)
    ]
    for copy in copies:
        copy.start()
    for copy in copies:
        copy.wait()


def hold(weights):
    return pl.pallas_call(
        hold_body,
        in_specs=[pl.BlockSpec(memory_space=pl.ANY)] * len(weights),
        out_specs=[VMEM] * len(weights),
        out_shape=[jax.ShapeDtypeStruct(w.shape, w.dtype) for w in weights],
        scratch_shapes=[pltpu.SemaphoreType.DMA((len(weights),))],
        compiler_params=SMALL,
        name="hold",
    )(*weights)


def sort_body(*refs):
    source = lax.broadcasted_iota(jnp.int32, (96, 48), 1)
    target = lax.broadcasted_iota(jnp.int32, (96, 48), 0)
    kind, slot = (source // CAP) & 1, source % CAP
    for half in range(2):
        total = 0.0
        for step in range(4):
            goal = kind * PIECE + step * CAP + slot
            pick = jnp.where(source // 24 == half, goal, -1) == target
            total = total + jnp.dot(
                jnp.where(pick, 1.0, 0.0).astype(jnp.bfloat16),
                refs[step][...],
                preferred_element_type=jnp.float32,
            )
        refs[4 + half][...] = total.astype(jnp.bfloat16)


def sort_rows(parts):
    return pl.pallas_call(
        sort_body,
        in_specs=[VMEM] * 4,
        out_specs=[VMEM] * 2,
        out_shape=[jax.ShapeDtypeStruct((96, BLOCK), jnp.bfloat16)] * 2,
        compiler_params=SMALL,
        name="sort_rows",
    )(*parts)


def tail_columns(product, rows):
    lane = lax.broadcasted_iota(jnp.int32, (rows, 128), 1)
    high = product.astype(jnp.bfloat16).astype(jnp.float32)
    return jnp.where(lane == 0, high, jnp.where(lane == 1, product - high, 0.0))


def collect_body(count, *refs):
    blocks, outs = refs[:count], refs[count:]
    rows = blocks[0].shape[0] - TAIL
    total = sum(block[...].astype(jnp.float32) for block in blocks)
    square = (rows, rows)
    diagonal = lax.broadcasted_iota(jnp.int32, square, 0) == lax.broadcasted_iota(jnp.int32, square, 1)
    line = total[rows : rows + 1, :rows] + total[rows + 1 : rows + 2, :rows]
    column = jnp.sum(jnp.where(diagonal, line, 0.0), axis=1, keepdims=True)
    tail = tail_columns(column, rows)
    for at, out in enumerate(outs):
        part = slice(at * PIECE, (at + 1) * PIECE)
        out[:, :BLOCK] = total[part].astype(out.dtype)
        out[:, BLOCK:] = tail[part].astype(out.dtype)


def collect(blocks, types):
    return pl.pallas_call(
        functools.partial(collect_body, len(blocks)),
        in_specs=[VMEM] * len(blocks),
        out_specs=[VMEM] * len(types),
        out_shape=[jax.ShapeDtypeStruct((PIECE, WIDE), t) for t in types],
        compiler_params=SMALL,
        name="collect",
    )(*blocks)


def homeward_body(*refs):
    f32, bf16 = jnp.float32, jnp.bfloat16
    rows = []
    for half in range(2):
        total = sum(refs[4 * half + at][...].astype(f32) for at in range(4))
        product = total[:, BLOCK : BLOCK + 1] + total[:, BLOCK + 1 : BLOCK + 2]
        rows.append((total[:, :BLOCK].astype(bf16), tail_columns(product, PIECE).astype(bf16)))
    source = lax.broadcasted_iota(jnp.int32, (32, PIECE), 1)
    target = lax.broadcasted_iota(jnp.int32, (32, PIECE), 0)
    for step in range(4):
        out = refs[8 + step]
        picks = [
            jnp.where(
                jnp.where(source // CAP == step, half * CAP + source % CAP, -1) == target, 1.0, 0.0
            ).astype(bf16)
            for half in range(2)
        ]
        for part, lanes in ((0, slice(0, BLOCK)), (1, slice(BLOCK, WIDE))):
            out[:, lanes] = sum(
                jnp.dot(picks[half], rows[half][part], preferred_element_type=f32) for half in range(2)
            ).astype(bf16)


def homeward(parts):
    return pl.pallas_call(
        homeward_body,
        in_specs=[VMEM] * 8,
        out_specs=[VMEM] * 4,
        out_shape=[jax.ShapeDtypeStruct((32, WIDE), jnp.bfloat16)] * 4,
        compiler_params=SMALL,
        name="homeward",
    )(*parts)


def plan_body(spot_ref, quota_ref, choices_ref, mixing_ref, *outs):
    f32, bf16 = jnp.float32, jnp.bfloat16
    lane = lax.broadcasted_iota(jnp.int32, (1, 128), 1)
    inner = lane & 31
    half = jnp.where(inner < CAP, 0, 1)
    slot = jnp.where(inner < 2 * CAP, inner - half * CAP, 1 << 20)
    picks = seats(spot_ref, quota_ref, choices_ref[...], lane >> 5, half, slot)
    weight = sum(picks[k] * as_column(mixing_ref[k : k + 1, :]) for k in range(2))
    for at in range(3):
        piece = weight.astype(bf16)
        weight = weight - piece.astype(f32)
        outs[at][...] = piece
    for k in range(2):
        outs[3 + k][...] = picks[k].astype(bf16)


def plan(spot, quota, choices, mixing):
    return pl.pallas_call(
        plan_body,
        in_specs=[SMEM] + [VMEM] * 3,
        out_specs=[VMEM] * 5,
        out_shape=[jax.ShapeDtypeStruct((128, 128), jnp.bfloat16)] * 5,
        compiler_params=SMALL,
        name="plan",
    )(spot, quota, choices, mixing)


def finish_body(*refs):
    f32, bf16 = jnp.float32, jnp.bfloat16
    plans, parts, (token_ref, gate_ref) = refs[:5], refs[5:9], refs[9:]
    tails = jnp.concatenate([part[:, BLOCK:] for part in parts], axis=0)
    rows = jnp.concatenate([part[:, :BLOCK] for part in parts], axis=0)
    total = sum(jnp.dot(plans[at][...], rows, preferred_element_type=f32) for at in range(3))
    token_ref[...] = total.astype(bf16)
    for k in range(2):
        found = lax.dot_general(
            tails, plans[3 + k][...], (((0,), (1,)), ((), ())), preferred_element_type=f32
        )
        gate_ref[k : k + 1, :] = found[0:1, :] + found[1:2, :]


def finish(plans, parts):
    return pl.pallas_call(
        finish_body,
        in_specs=[VMEM] * 9,
        out_specs=[VMEM] * 2,
        out_shape=[
            jax.ShapeDtypeStruct((128, BLOCK), jnp.bfloat16),
            jax.ShapeDtypeStruct((2, 128), jnp.float32),
        ],
        compiler_params=SMALL,
        name="finish",
    )(*plans, *parts)


def local(
    layer_activations_input,
    output_gradient,
    specialist_choices_matrix,
    mixing_coefficients,
    quota_table,
    gating_matrix,
    widening_matrix,
    contracting_matrix,
):
    f32, bf16 = jnp.float32, jnp.bfloat16
    barrier = lax.optimization_barrier
    own = lax.axis_index("ed").astype(jnp.int32)
    spot = jnp.stack([lax.axis_index("tp").astype(jnp.int32), own >> 4, (own >> 3) & 1])
    own_weights = (gating_matrix, widening_matrix, contracting_matrix)
    gating, widening, spot = barrier((gating_matrix, widening_matrix, spot))
    other_gate, other_up = across_cores(gating), across_cores(widening)

    choices = specialist_choices_matrix.T
    payload = front(spot, quota_table, choices, layer_activations_input, output_gradient)
    arrived = [payload[0]] + [along_y(payload[step], step) for step in (1, 2, 3)]
    *arrived, other_gate, other_up, contracting = barrier(
        (*arrived, other_gate, other_up, contracting_matrix)
    )
    other_down = across_cores(contracting)
    same, other = sort_rows(arrived)
    plans = plan(spot, quota_table, choices, mixing_coefficients.T)

    def opposite(left, right):
        middle = left.shape[0] // 2
        return along_x(left[:middle], 1), along_x(right[middle:], -1)

    near = [same, along_z(same, 1), along_z(other, 4), along_z(other, 5)]
    distant = [along_z(same, 2), along_z(same, 3), along_z(other, 6), along_z(other, 7)]
    block1 = jnp.concatenate(near, axis=0)
    block1, other_down, held, plans = barrier((block1, other_down, hold(own_weights[1:]), plans))
    own_weights = (gating_matrix, *held)
    left1, right1 = along_x(block1, 1), along_x(block1, -1)
    block2 = jnp.concatenate(distant, axis=0)
    block2, left1, right1 = barrier((block2, left1, right1))
    left2, right2 = along_x(block2, 1), along_x(block2, -1)
    groups1, far1 = [(block1, left1, right1)], opposite(left1, right1)
    other_weights = (other_gate, other_up, other_down)
    first = expert(spot, groups1, far1, own_weights, other_weights)
    mine, to_left, to_right, to_far = first
    middle = 2 * PIECE
    passing = [along_x(to_far[:middle], 1), along_x(to_far[middle:], -1)]
    left2, right2, mine, to_left, to_right = barrier((left2, right2, mine, to_left, to_right))
    far2 = opposite(left2, right2)
    low = (to_right[:middle].astype(f32) + passing[0].astype(f32)).astype(bf16)
    high = (to_left[middle:].astype(f32) + passing[1].astype(f32)).astype(bf16)
    to_right = jnp.concatenate([low, to_right[middle:]], axis=0)
    to_left = jnp.concatenate([to_left[:middle], high], axis=0)
    *far2, to_right, to_left = barrier((*far2, to_right, to_left))
    second = expert(spot, [(block2, left2, right2)], far2, own_weights, other_weights)

    back1 = collect((mine, along_x(to_left, -1), along_x(to_right, 1)), (f32, bf16, bf16, bf16))
    back1 = [back1[0]] + [along_z(part, flip) for part, flip in zip(back1[1:], (1, 4, 5))]
    mine, to_left, to_right, to_far = second
    back2 = collect(
        (mine, along_x(to_far, 2), along_x(to_left, -1), along_x(to_right, 1)), (bf16,) * 4
    )
    back2 = [along_z(part, flip) for part, flip in zip(back2, (2, 3, 6, 7))]
    same_rows = (back1[0], back1[1], back2[0], back2[1])
    other_rows = (back1[2], back1[3], back2[2], back2[3])
    returned = homeward((*same_rows, *other_rows))
    home = [returned[0]] + [along_y(returned[step], -step) for step in (1, 2, 3)]
    token_grads, gate_grads = finish(plans, home)
    return token_grads, gate_grads.T


def solution(mesh):
    in_specs = (
        P("ed", "tp"),
        P("ed", "tp"),
        P("ed", None),
        P("ed", None),
        P("ed", None),
        P(None, ("ed", "tp")),
        P(None, ("ed", "tp")),
        P(("ed", "tp"), None),
    )
    out_specs = (P("ed", "tp"), P("ed", None))
    return jax.shard_map(local, mesh=mesh, in_specs=in_specs, out_specs=out_specs, check_vma=False)
```
